32 devices in a mesh: cell: 8 (over y, x, core), state: 4 (over z).
Axes of the slice: x: 2, y: 2, z: 4, core: 2. Of those that a mesh axis runs over, the one named last changes fastest.
Arguments:
- start_block: float32 [1024, 4096], P('state', 'cell'), may hold values from -6 to 6
- connectivity: int32 [16, 343], P('cell'), may hold values from 0 to 575, as said below
- cell_matrices: bfloat16 [16, 343, 343], P('cell'), may hold values from -4 to 4
- bounds: float32 [3], replicated, may hold values from -1 to 32, as said below
Outputs:
- filtered: float32 [1024, 4096], P('state', 'cell')
- projected: float32 [1024, 1024], P('cell', 'state')
The draws below stay inside these ranges and needn't reach their ends.
Inputs may be any that keep to these rules, and one draw needn't show every extreme that they name: `connectivity`: each row names 343 different local nodes; numbers below 512 are nodes owned by the index of cell that holds the cell, the others the first 64 nodes of the next index of cell, cyclically. `bounds`: lowest < cut < upper, and every eigenvalue of H lies above lowest.
All inputs are finite; a program needn't handle non-finite values.
Results may differ from the reference program's by a relative error of at most 0.0016.
Values may be sent and summed in bfloat16 or wider, within the bound.
A program may use at most 64 MiB of HBM per device.

```python
import jax
import jax.numpy as jnp
from jax import lax

NSTATES = 1024
NPC = 343
DEGREE = 8
CELLS_DEV = 2
NODE_DEV = 512
HALO = 64
NCELLS = 16
NODES = 4096
N_CELL = 8


def draw_connectivity(key, part):
    extent = NODE_DEV + HALO
    scores = jax.random.randint(key, (NCELLS, extent), 0, 2 ** 20) * extent + jnp.arange(extent, dtype=jnp.int32)[None, :]
    order = jnp.argsort(scores, axis=1, stable=True)
    return order[:, :NPC].astype(jnp.int32)


def draw_cell_matrices(key, part):
    key_off = jax.random.fold_in(key, 11)
    key_diag = jax.random.fold_in(key, 12)
    noise = jax.random.normal(key_off, (NCELLS, NPC, NPC), jnp.float32)
    diag = jax.random.uniform(key_diag, (NCELLS, NPC), jnp.float32, 1.5, 3.5)
    sym = (noise + jnp.swapaxes(noise, 1, 2)) * (0.5 / jnp.sqrt(2.0 * NPC))
    eye = jnp.eye(NPC, dtype=jnp.float32)
    matrix = sym * (1.0 - eye)[None] + diag[:, :, None] * eye[None]
    return matrix.astype(jnp.bfloat16)


def draw_bounds(key, part):
    parts = jax.random.uniform(key, (3,), jnp.float32, 0.0, 1.0)
    lowest = -1.0 + 0.5 * parts[0]
    cut = 4.0 + 2.0 * parts[1]
    upper = 28.0 + 4.0 * parts[2]
    return jnp.stack([lowest, cut, upper]).astype(jnp.float32)


def shard_levels(stream_key, shape, split, low, largest):
    factor_of = 1.0
    for position, shards_of in split:
        steps = jax.random.uniform(jax.random.fold_in(jax.random.fold_in(stream_key, 6), position), (shards_of,), jnp.float32, low / len(split), largest / len(split))
        factor_of = factor_of * jnp.repeat(jnp.exp(steps), shape[position] // shards_of).reshape((-1,) + (1,) * (len(shape) - 1 - position))
    return factor_of


def centred(key, dims, deviation, limit, split=(), held_as=jnp.bfloat16):
    gain = shard_levels(key, dims, split, -0.22, 0.18) if split else 1.0
    array = jax.random.normal(key, dims, jnp.float32) * deviation * gain
    return jnp.minimum(jnp.maximum(array, -limit), limit).astype(held_as)


def setup_inputs(seed: int = 0) -> dict:
    key_list = jax.random.split(jax.random.key(seed), 5)
    return {
        "start_block": centred(key_list[0], (NSTATES, NODES), 1.0, 6.0, ((0, 4), (1, 8)), jnp.float32),
        "connectivity": draw_connectivity(jax.random.fold_in(key_list[4], 71), 0),
        "cell_matrices": draw_cell_matrices(jax.random.fold_in(key_list[4], 71), 0),
        "bounds": draw_bounds(jax.random.fold_in(key_list[4], 71), 0),
    }


def apply_operator(field, connectivity, cell_matrices):
    states = field.shape[0]
    blocks = field.astype(jnp.bfloat16).reshape(states, N_CELL, NODE_DEV).transpose(1, 0, 2)
    ghost = jnp.roll(blocks[:, :, :HALO], -1, axis=0)
    extended = jnp.concatenate([blocks, ghost], axis=2)
    links = connectivity.reshape(N_CELL, CELLS_DEV, NPC)
    locals_ = cell_matrices.reshape(N_CELL, CELLS_DEV, NPC, NPC)

    def one_index(item):
        ext, link, matrix = item
        picked = ext[:, link].astype(jnp.float32)
        product = jnp.einsum("scj,ckj->sck", picked, matrix.astype(jnp.float32), precision=lax.Precision.HIGHEST)
        return jnp.zeros(ext.shape, jnp.float32).at[:, link].add(product)

    sums = lax.map(one_index, (extended, links, locals_))
    owned = sums[:, :, :NODE_DEV]
    incoming = jnp.roll(sums[:, :, NODE_DEV:], 1, axis=0)
    owned = owned.at[:, :, :HALO].add(incoming)
    return owned.transpose(1, 0, 2).reshape(states, N_CELL * NODE_DEV)


def reference(start_block, connectivity, cell_matrices, bounds):
    lowest, cut, upper = bounds[0], bounds[1], bounds[2]
    half = (upper - cut) / 2.0
    centre = (upper + cut) / 2.0
    sigma = half / (lowest - centre)
    tau = 2.0 / sigma
    previous = start_block
    current = (apply_operator(start_block, connectivity, cell_matrices) - centre * start_block) * (sigma / half)
    for degree in range(2, DEGREE + 1):
        sigma_new = 1.0 / (tau - sigma)
        upcoming = (apply_operator(current, connectivity, cell_matrices) - centre * current) * (2.0 * sigma_new / half) - (sigma * sigma_new) * previous
        previous = current
        current = upcoming
        sigma = sigma_new
    low = current.astype(jnp.bfloat16)
    image = apply_operator(current, connectivity, cell_matrices).astype(jnp.bfloat16)
    projected = jnp.dot(low, image.T, preferred_element_type=jnp.float32)
    return current, projected
```

```python
import functools

import jax
import jax.numpy as jnp
from jax import lax
from jax.experimental import pallas as pl
from jax.experimental.pallas import tpu as pltpu
from jax.sharding import PartitionSpec as P

DEGREE = 8
MESH = pl.DeviceIdType.MESH


def matmul(left, right):
    return jnp.dot(left, right, preferred_element_type=jnp.float32)


def filter_kernel(
    count, start, links, cells, bounds, filtered, low, image,
    matrix, stack, field, before, inner, outgoing, incoming, ghost, sends, receives, ghost_sems,
):
    states, owned = start.shape
    shared = owned // 8
    both = 2 * shared
    extent = owned + shared
    rest = extent - both
    first = 2 * both
    second = first + (rest + 127) // 128 * 128
    me = lax.axis_index("cell")
    right, left = lax.rem(me + 1, count), lax.rem(me + count - 1, count)

    barrier = pltpu.get_barrier_semaphore()
    for neighbour in (left, right):
        pl.semaphore_signal(barrier, inc=1, device_id={"cell": neighbour}, device_id_type=MESH)

    field[0:both, :] = start[:, 0:both].T
    stack[0:both, :] = field[0:both, :].astype(jnp.bfloat16)
    pl.semaphore_wait(barrier, 2)
    ghost_copy = pltpu.make_async_remote_copy(
        src_ref=outgoing.at[pl.ds(0, shared)],
        dst_ref=ghost,
        send_sem=ghost_sems.at[0],
        recv_sem=ghost_sems.at[1],
        device_id={"cell": left},
        device_id_type=MESH,
    )
    outgoing[0:shared, :] = field[0:shared, :]
    ghost_copy.start()

    whole = start[...].T
    field[both:, :] = whole[shared:, :]
    before[...] = jnp.zeros_like(before)

    for cell in range(links.shape[0]):
        link = links[cell : cell + 1, :]
        row = jnp.where(
            link < shared, link, jnp.where(link < owned, link + shared, link - (owned - shared))
        )
        spread = lax.broadcasted_iota(jnp.int32, (extent, links.shape[1]), 0) == row
        spread = jnp.where(spread, 1.0, 0.0).astype(jnp.bfloat16)
        half_way = matmul(spread, cells[cell]).astype(jnp.bfloat16)
        placed = lax.dot_general(
            half_way, spread, (((1,), (1,)), ((), ())), preferred_element_type=jnp.float32
        ).astype(jnp.bfloat16)
        matrix[:, cell * both : (cell + 1) * both] = placed[:, 0:both]
        begin = first if cell == 0 else second
        matrix[:, begin : begin + rest] = placed[:, both:]
    if second > first + rest:
        matrix[:, first + rest : second] = jnp.zeros((extent, second - first - rest), jnp.bfloat16)
        stack[first + rest : second, :] = jnp.zeros((second - first - rest, states), jnp.bfloat16)

    def put_rest():
        rounded = field[both:, :].astype(jnp.bfloat16)
        stack[first : first + rest, :] = rounded
        stack[second : second + rest, :] = rounded
        inner[...] = matmul(matrix[0:both, first:], stack[first:, :])

    def put_shared():
        rounded = field[0:both, :].astype(jnp.bfloat16)
        stack[0:both, :] = rounded
        stack[both:first, :] = rounded
        outgoing[...] = inner[...] + matmul(matrix[0:both, 0:first], stack[0:first, :])

    def copies(slot):
        to_left = pltpu.make_async_remote_copy(
            src_ref=outgoing.at[pl.ds(0, shared)],
            dst_ref=incoming.at[slot, pl.ds(shared, shared)],
            send_sem=sends.at[0],
            recv_sem=receives.at[slot, 0],
            device_id={"cell": left},
            device_id_type=MESH,
        )
        to_right = pltpu.make_async_remote_copy(
            src_ref=outgoing.at[pl.ds(shared, shared)],
            dst_ref=incoming.at[slot, pl.ds(0, shared)],
            send_sem=sends.at[1],
            recv_sem=receives.at[slot, 1],
            device_id={"cell": right},
            device_id_type=MESH,
        )
        return to_left, to_right

    put_rest()
    ghost_copy.wait()
    field[shared:both, :] = ghost[...]
    put_shared()
    for copy in copies(0):
        copy.start()

    def vector(value):
        return jnp.full((1, states), value, jnp.float32)

    lowest, cut, upper = vector(bounds[0]), vector(bounds[1]), vector(bounds[2])
    half = (upper - cut) / 2.0
    centre = (upper + cut) / 2.0
    sigma_first = half / (lowest - centre)
    tau = 2.0 / sigma_first

    def degree_step(step, carry):
        alpha, beta, sigma = carry
        slot = lax.rem(step, 2)
        new_rest = (
            matmul(matrix[both:, :], stack[...]) - centre * field[both:, :]
        ) * alpha - beta * before[both:, :]
        before[both:, :] = field[both:, :]
        field[both:, :] = new_rest
        put_rest()
        for copy in copies(slot):
            copy.wait()
        new_shared = (
            outgoing[...] + incoming[slot] - centre * field[0:both, :]
        ) * alpha - beta * before[0:both, :]
        before[0:both, :] = field[0:both, :]
        field[0:both, :] = new_shared
        put_shared()
        for copy in copies(lax.rem(step + 1, 2)):
            copy.start()
        sigma_new = 1.0 / (tau - sigma)
        return 2.0 * sigma_new / half, sigma * sigma_new, sigma_new

    lax.fori_loop(
        0, DEGREE, degree_step, (sigma_first / half, jnp.zeros_like(half), sigma_first)
    )

    result = jnp.concatenate([field[0:shared, :], field[both:, :]], axis=0).T
    filtered[...] = result
    low[...] = result.astype(jnp.bfloat16)
    image[shared:, :] = matmul(matrix[both:, :], stack[...]).astype(jnp.bfloat16)
    last = DEGREE % 2
    for copy in copies(last):
        copy.wait()
    image[0:shared, :] = (outgoing[0:shared, :] + incoming[last, 0:shared, :]).astype(jnp.bfloat16)


def filtered_block(start, links, cells, bounds, count):
    states, owned = start.shape
    shared = owned // 8
    both = 2 * shared
    extent = owned + shared
    rest = extent - both
    depth = 2 * both + (rest + 127) // 128 * 128 + rest
    vmem = pl.BlockSpec(memory_space=pltpu.VMEM)
    return pl.pallas_call(
        functools.partial(filter_kernel, count),
        out_shape=(
            jax.ShapeDtypeStruct((states, owned), jnp.float32),
            jax.ShapeDtypeStruct((states, owned), jnp.bfloat16),
            jax.ShapeDtypeStruct((owned, states), jnp.bfloat16),
        ),
        in_specs=[vmem, vmem, vmem, pl.BlockSpec(memory_space=pltpu.SMEM)],
        out_specs=(vmem, vmem, vmem),
        scratch_shapes=[
            pltpu.VMEM((extent, depth), jnp.bfloat16),
            pltpu.VMEM((depth, states), jnp.bfloat16),
            pltpu.VMEM((extent, states), jnp.float32),
            pltpu.VMEM((extent, states), jnp.float32),
            pltpu.VMEM((both, states), jnp.float32),
            pltpu.VMEM((both, states), jnp.float32),
            pltpu.VMEM((2, both, states), jnp.float32),
            pltpu.VMEM((shared, states), jnp.float32),
            pltpu.SemaphoreType.DMA((2,)),
            pltpu.SemaphoreType.DMA((2, 2)),
            pltpu.SemaphoreType.DMA((2,)),
        ],
        compiler_params=pltpu.CompilerParams(
            collective_id=0, has_side_effects=True, vmem_limit_bytes=40 * 1024 * 1024
        ),
    )(start, links, cells, bounds)


def per_device(start_block, connectivity, cell_matrices, bounds, count):
    filtered, low, image = filtered_block(
        start_block, connectivity, cell_matrices, bounds, count
    )
    all_low = lax.all_gather(low, "state", axis=0, tiled=True)
    partial_value = matmul(all_low, image)
    projected = lax.psum_scatter(partial_value, "cell", scatter_dimension=0, tiled=True)
    return (filtered, projected)


def solution(mesh):
    in_specs = (P("state", "cell"), P("cell", None), P("cell", None, None), P())
    out_specs = (P("state", "cell"), P("cell", "state"))
    return jax.shard_map(
        functools.partial(per_device, count=mesh.shape["cell"]),
        mesh=mesh, in_specs=in_specs, out_specs=out_specs, check_vma=False,
    )
```

```python
import functools

import jax
import jax.numpy as jnp
from jax import lax
from jax.experimental import pallas as pl
from jax.experimental.pallas import tpu as pltpu
from jax.sharding import PartitionSpec as P

DEGREE = 8
MESH = pl.DeviceIdType.MESH


def matmul(left, right):
    return jnp.dot(left, right, preferred_element_type=jnp.float32)


def filter_kernel(
    count, groups, start, links, cells, bounds, filtered, projected,
    matrix, stack, field, before, inner, outgoing, rounded_out, incoming, ghost,
    image, lows, parts, swapped, ship, gathered, mine,
    sends, receives, ghost_sems, along_send, along_recv, swap_send, swap_recv,
    ship_send, ship_recv,
):
    states, owned = start.shape
    shared = owned // 8
    both = 2 * shared
    extent = owned + shared
    rest = extent - both
    first = 2 * both
    second = first + (rest + 127) // 128 * 128
    me = lax.axis_index("cell")
    right, left = lax.rem(me + 1, count), lax.rem(me + count - 1, count)

    rows = projected.shape[0]
    owners = states // rows
    chips = count // 2
    chip, core = me // 2, lax.rem(me, 2)
    place = lax.axis_index("state")

    barrier = pltpu.get_barrier_semaphore()

    def greet(target):
        pl.semaphore_signal(barrier, inc=1, device_id=target, device_id_type=MESH)

    greet({"cell": left})
    greet({"cell": right})
    for other in range(chips):

        @pl.when(other != chip)
        def _():
            greet({"cell": 2 * other + core})

    @pl.when(place > 0)
    def _():
        greet({"state": place - 1})

    @pl.when(place < groups - 1)
    def _():
        greet({"state": place + 1})

    field[0:both, :] = start[:, 0:both].T
    stack[0:both, :] = field[0:both, :].astype(jnp.bfloat16)
    beside = jnp.minimum(place, 1) + jnp.minimum(groups - 1 - place, 1)
    pl.semaphore_wait(barrier, 1 + chips + beside)
    ghost_copy = pltpu.make_async_remote_copy(
        src_ref=outgoing.at[pl.ds(0, shared)],
        dst_ref=ghost,
        send_sem=ghost_sems.at[0],
        recv_sem=ghost_sems.at[1],
        device_id={"cell": left},
        device_id_type=MESH,
    )
    outgoing[0:shared, :] = field[0:shared, :]
    ghost_copy.start()

    whole = start[...].T
    field[both:, :] = whole[shared:, :]
    before[...] = jnp.zeros_like(before)

    for cell in range(links.shape[0]):
        link = links[cell : cell + 1, :]
        row = jnp.where(
            link < shared, link, jnp.where(link < owned, link + shared, link - (owned - shared))
        )
        spread = lax.broadcasted_iota(jnp.int32, (extent, links.shape[1]), 0) == row
        spread = jnp.where(spread, 1.0, 0.0).astype(jnp.bfloat16)
        half_way = matmul(spread, cells[cell]).astype(jnp.bfloat16)
        placed = lax.dot_general(
            half_way, spread, (((1,), (1,)), ((), ())), preferred_element_type=jnp.float32
        ).astype(jnp.bfloat16)
        matrix[:, cell * both : (cell + 1) * both] = placed[:, 0:both]
        begin = first if cell == 0 else second
        matrix[:, begin : begin + rest] = placed[:, both:]
    if second > first + rest:
        matrix[:, first + rest : second] = jnp.zeros((extent, second - first - rest), jnp.bfloat16)
        stack[first + rest : second, :] = jnp.zeros((second - first - rest, states), jnp.bfloat16)

    def put_rest():
        rounded = field[both:, :].astype(jnp.bfloat16)
        stack[first : first + rest, :] = rounded
        stack[second : second + rest, :] = rounded
        inner[...] = matmul(matrix[0:both, first:], stack[first:, :])

    def put_shared():
        rounded = field[0:both, :].astype(jnp.bfloat16)
        stack[0:both, :] = rounded
        stack[both:first, :] = rounded
        total = inner[...] + matmul(matrix[0:both, 0:first], stack[0:first, :])
        outgoing[...] = total
        rounded_out[...] = total.astype(jnp.bfloat16)

    def copies(slot):
        to_left = pltpu.make_async_remote_copy(
            src_ref=rounded_out.at[pl.ds(0, shared)],
            dst_ref=incoming.at[slot, pl.ds(shared, shared)],
            send_sem=sends.at[0],
            recv_sem=receives.at[slot, 0],
            device_id={"cell": left},
            device_id_type=MESH,
        )
        to_right = pltpu.make_async_remote_copy(
            src_ref=rounded_out.at[pl.ds(shared, shared)],
            dst_ref=incoming.at[slot, pl.ds(0, shared)],
            send_sem=sends.at[1],
            recv_sem=receives.at[slot, 1],
            device_id={"cell": right},
            device_id_type=MESH,
        )
        return to_left, to_right

    put_rest()
    ghost_copy.wait()
    field[shared:both, :] = ghost[...]
    put_shared()
    for copy in copies(0):
        copy.start()

    def vector(value):
        return jnp.full((1, states), value, jnp.float32)

    lowest, cut, upper = vector(bounds[0]), vector(bounds[1]), vector(bounds[2])
    half = (upper - cut) / 2.0
    centre = (upper + cut) / 2.0
    sigma_first = half / (lowest - centre)
    tau = 2.0 / sigma_first

    def degree_step(step, carry):
        alpha, beta, sigma = carry
        slot = lax.rem(step, 2)
        new_rest = (
            matmul(matrix[both:, :], stack[...]) - centre * field[both:, :]
        ) * alpha - beta * before[both:, :]
        before[both:, :] = field[both:, :]
        field[both:, :] = new_rest
        put_rest()
        for copy in copies(slot):
            copy.wait()
        new_shared = (
            outgoing[...] + incoming[slot] - centre * field[0:both, :]
        ) * alpha - beta * before[0:both, :]
        before[0:both, :] = field[0:both, :]
        field[0:both, :] = new_shared
        put_shared()
        for copy in copies(lax.rem(step + 1, 2)):
            copy.start()
        sigma_new = 1.0 / (tau - sigma)
        return 2.0 * sigma_new / half, sigma * sigma_new, sigma_new

    lax.fori_loop(
        0, DEGREE, degree_step, (sigma_first / half, jnp.zeros_like(half), sigma_first)
    )

    result = jnp.concatenate([field[0:shared, :], field[both:, :]], axis=0).T
    filtered[...] = result
    lows[place] = result.astype(jnp.bfloat16)

    def hand_on(way, hop):
        step = 1 - 2 * way
        block = lax.rem(place - step * hop + groups, groups)
        return pltpu.make_async_remote_copy(
            src_ref=lows.at[block],
            dst_ref=lows.at[block],
            send_sem=along_send.at[way, hop],
            recv_sem=along_recv.at[way, hop],
            device_id={"state": lax.rem(place + step + groups, groups)},
            device_id_type=MESH,
        )

    def sends_at(way, hop):
        if way == 0:
            return jnp.logical_and(place < groups - 1, place >= hop)
        return jnp.logical_and(place > 0, place + hop < groups)

    def receives_at(way, hop):
        if way == 0:
            return place >= hop + 1
        return place + hop + 1 < groups

    def block_at(way, hop):
        return lax.rem(place - (1 - 2 * way) * (hop + 1) + groups, groups)

    def arrival(way, hop):
        step = 1 - 2 * way
        block = block_at(way, hop)
        return pltpu.make_async_remote_copy(
            src_ref=lows.at[block],
            dst_ref=lows.at[block],
            send_sem=along_send.at[way, hop],
            recv_sem=along_recv.at[way, hop],
            device_id={"state": lax.rem(place + step + groups, groups)},
            device_id_type=MESH,
        )

    for way in range(2):

        @pl.when(sends_at(way, 0))
        def _():
            hand_on(way, 0).start()

    image[shared:, :] = matmul(matrix[both:, :], stack[...]).astype(jnp.bfloat16)
    last = DEGREE % 2
    for copy in copies(last):
        copy.wait()
    image[0:shared, :] = (outgoing[0:shared, :] + incoming[last, 0:shared, :]).astype(jnp.bfloat16)

    def swap(block, pair):
        return pltpu.make_async_remote_copy(
            src_ref=parts.at[block, pl.ds((2 * pair + 1 - core) * rows, rows)],
            dst_ref=swapped.at[block, pl.ds(pair * rows, rows)],
            send_sem=swap_send.at[block, pair],
            recv_sem=swap_recv.at[block, pair],
            device_id={"cell": chip * 2 + 1 - core},
            device_id_type=MESH,
        )

    def owner_of(block, pair):
        return block * (owners // 2) + pair

    def shipping(block, pair):
        return pltpu.make_async_remote_copy(
            src_ref=ship.at[block, pl.ds(pair * rows, rows)],
            dst_ref=gathered.at[chip],
            send_sem=ship_send.at[block, pair],
            recv_sem=ship_recv.at[chip],
            device_id={"cell": 2 * owner_of(block, pair) + core},
            device_id_type=MESH,
        )

    def multiply(block):
        parts[block] = matmul(lows[block], image[...])
        for pair in range(owners // 2):
            swap(block, pair).start()

    def pass_to_owners(block):
        for pair in range(owners // 2):
            swap(block, pair).wait()
            kept = pl.ds(pl.multiple_of((2 * pair + core) * rows, rows), rows)
            total = parts[block, kept, :] + swapped[block, pair * rows : (pair + 1) * rows, :]

            @pl.when(owner_of(block, pair) == chip)
            def _():
                mine[...] = total

            @pl.when(owner_of(block, pair) != chip)
            def _():
                ship[block, pair * rows : (pair + 1) * rows, :] = total.astype(jnp.bfloat16)
                shipping(block, pair).start()

    multiply(place)
    pass_to_owners(place)
    for hop in range(groups - 1):
        for way in range(2):

            @pl.when(receives_at(way, hop))
            def _():
                arrival(way, hop).wait_recv()
                if hop + 1 < groups - 1:

                    @pl.when(sends_at(way, hop + 1))
                    def _():
                        hand_on(way, hop + 1).start()

                multiply(block_at(way, hop))

        for way in range(2):

            @pl.when(receives_at(way, hop))
            def _():
                pass_to_owners(block_at(way, hop))

    for way in range(2):
        for hop in range(groups - 1):

            @pl.when(sends_at(way, hop))
            def _():
                hand_on(way, hop).wait_send()

    for block in range(groups):
        for pair in range(owners // 2):

            @pl.when(owner_of(block, pair) != chip)
            def _():
                shipping(block, pair).wait_send()

    for other in range(chips):

        @pl.when(other != chip)
        def _():
            pltpu.make_async_remote_copy(
                src_ref=gathered.at[other],
                dst_ref=gathered.at[other],
                send_sem=ship_send.at[0, 0],
                recv_sem=ship_recv.at[other],
                device_id={"cell": 2 * other + core},
                device_id_type=MESH,
            ).wait_recv()
            mine[...] += gathered[other].astype(jnp.float32)

    projected[...] = mine[...]


def filtered_block(start, links, cells, bounds, count, groups):
    states, owned = start.shape
    shared = owned // 8
    both = 2 * shared
    extent = owned + shared
    rest = extent - both
    depth = 2 * both + (rest + 127) // 128 * 128 + rest
    rows = states * groups // count
    pairs = states // rows // 2
    chips = count // 2
    vmem = pl.BlockSpec(memory_space=pltpu.VMEM)
    dma = pltpu.SemaphoreType.DMA
    return pl.pallas_call(
        functools.partial(filter_kernel, count, groups),
        out_shape=(
            jax.ShapeDtypeStruct((states, owned), jnp.float32),
            jax.ShapeDtypeStruct((rows, states), jnp.float32),
        ),
        in_specs=[vmem, vmem, vmem, pl.BlockSpec(memory_space=pltpu.SMEM)],
        out_specs=(vmem, vmem),
        scratch_shapes=[
            pltpu.VMEM((extent, depth), jnp.bfloat16),
            pltpu.VMEM((depth, states), jnp.bfloat16),
            pltpu.VMEM((extent, states), jnp.float32),
            pltpu.VMEM((extent, states), jnp.float32),
            pltpu.VMEM((both, states), jnp.float32),
            pltpu.VMEM((both, states), jnp.float32),
            pltpu.VMEM((both, states), jnp.bfloat16),
            pltpu.VMEM((2, both, states), jnp.bfloat16),
            pltpu.VMEM((shared, states), jnp.float32),
            pltpu.VMEM((owned, states), jnp.bfloat16),
            pltpu.VMEM((groups, states, owned), jnp.bfloat16),
            pltpu.VMEM((groups, states, states), jnp.float32),
            pltpu.VMEM((groups, pairs * rows, states), jnp.float32),
            pltpu.VMEM((groups, pairs * rows, states), jnp.bfloat16),
            pltpu.VMEM((chips, rows, states), jnp.bfloat16),
            pltpu.VMEM((rows, states), jnp.float32),
            dma((2,)),
            dma((2, 2)),
            dma((2,)),
            dma((2, groups)),
            dma((2, groups)),
            dma((groups, pairs)),
            dma((groups, pairs)),
            dma((groups, pairs)),
            dma((chips,)),
        ],
        compiler_params=pltpu.CompilerParams(
            collective_id=0, has_side_effects=True, vmem_limit_bytes=40 * 1024 * 1024
        ),
    )(start, links, cells, bounds)


def solution(mesh):
    in_specs = (P("state", "cell"), P("cell", None), P("cell", None, None), P())
    out_specs = (P("state", "cell"), P("cell", "state"))
    return jax.shard_map(
        functools.partial(
            filtered_block, count=mesh.shape["cell"], groups=mesh.shape["state"]
        ),
        mesh=mesh, in_specs=in_specs, out_specs=out_specs, check_vma=False,
    )
```

```python
import functools

import jax
import jax.numpy as jnp
from jax import lax
from jax.experimental import pallas as pl
from jax.experimental.pallas import tpu as pltpu
from jax.sharding import PartitionSpec as P

DEGREE = 8
MESH = pl.DeviceIdType.MESH


def matmul(left, right):
    return jnp.dot(left, right, preferred_element_type=jnp.float32)


def filter_kernel(
    count, groups, start, links, cells, bounds, filtered, projected,
    matrix, stack, field, before, inner, outgoing, rounded_out, incoming, ghost,
    image, lows, parts, swapped, ship, gathered, mine,
    sends, receives, ghost_sems, along_send, along_recv, swap_send, swap_recv,
    ship_send, ship_recv,
):
    states, owned = start.shape
    shared = owned // 8
    both = 2 * shared
    extent = owned + shared
    rest = extent - both
    first = 2 * both
    second = first + (rest + 127) // 128 * 128
    me = lax.axis_index("cell")
    right, left = lax.rem(me + 1, count), lax.rem(me + count - 1, count)

    rows = projected.shape[0]
    owners = states // rows
    chips = count // 2
    chip, core = me // 2, lax.rem(me, 2)
    place = lax.axis_index("state")

    barrier = pltpu.get_barrier_semaphore()

    def greet(target):
        pl.semaphore_signal(barrier, inc=1, device_id=target, device_id_type=MESH)

    greet({"cell": left})
    greet({"cell": right})
    for other in range(chips):

        @pl.when(other != chip)
        def _():
            greet({"cell": 2 * other + core})

    @pl.when(place > 0)
    def _():
        greet({"state": place - 1})

    @pl.when(place < groups - 1)
    def _():
        greet({"state": place + 1})

    field[0:both, :] = start[:, 0:both].T
    stack[0:both, :] = field[0:both, :].astype(jnp.bfloat16)
    beside = jnp.minimum(place, 1) + jnp.minimum(groups - 1 - place, 1)
    pl.semaphore_wait(barrier, 1 + chips + beside)
    ghost_copy = pltpu.make_async_remote_copy(
        src_ref=outgoing.at[pl.ds(0, shared)],
        dst_ref=ghost,
        send_sem=ghost_sems.at[0],
        recv_sem=ghost_sems.at[1],
        device_id={"cell": left},
        device_id_type=MESH,
    )
    outgoing[0:shared, :] = field[0:shared, :]
    ghost_copy.start()

    whole = start[...].T
    field[both:, :] = whole[shared:, :]
    before[...] = jnp.zeros_like(before)

    for cell in range(links.shape[0]):
        link = links[cell : cell + 1, :]
        row = jnp.where(
            link < shared, link, jnp.where(link < owned, link + shared, link - (owned - shared))
        )
        spread = lax.broadcasted_iota(jnp.int32, (extent, links.shape[1]), 0) == row
        spread = jnp.where(spread, 1.0, 0.0).astype(jnp.bfloat16)
        half_way = matmul(spread, cells[cell]).astype(jnp.bfloat16)
        placed = lax.dot_general(
            half_way, spread, (((1,), (1,)), ((), ())), preferred_element_type=jnp.float32
        ).astype(jnp.bfloat16)
        matrix[:, cell * both : (cell + 1) * both] = placed[:, 0:both]
        begin = first if cell == 0 else second
        matrix[:, begin : begin + rest] = placed[:, both:]
    if second > first + rest:
        matrix[:, first + rest : second] = jnp.zeros((extent, second - first - rest), jnp.bfloat16)
        stack[first + rest : second, :] = jnp.zeros((second - first - rest, states), jnp.bfloat16)

    def put_rest():
        rounded = field[both:, :].astype(jnp.bfloat16)
        stack[first : first + rest, :] = rounded
        stack[second : second + rest, :] = rounded
        inner[...] = matmul(matrix[0:both, first:], stack[first:, :])

    def put_shared():
        rounded = field[0:both, :].astype(jnp.bfloat16)
        stack[0:both, :] = rounded
        stack[both:first, :] = rounded
        total = inner[...] + matmul(matrix[0:both, 0:first], stack[0:first, :])
        outgoing[...] = total
        rounded_out[...] = total.astype(jnp.bfloat16)

    def copies(slot):
        to_left = pltpu.make_async_remote_copy(
            src_ref=rounded_out.at[pl.ds(0, shared)],
            dst_ref=incoming.at[slot, pl.ds(shared, shared)],
            send_sem=sends.at[0],
            recv_sem=receives.at[slot, 0],
            device_id={"cell": left},
            device_id_type=MESH,
        )
        to_right = pltpu.make_async_remote_copy(
            src_ref=rounded_out.at[pl.ds(shared, shared)],
            dst_ref=incoming.at[slot, pl.ds(0, shared)],
            send_sem=sends.at[1],
            recv_sem=receives.at[slot, 1],
            device_id={"cell": right},
            device_id_type=MESH,
        )
        return to_left, to_right

    put_rest()
    ghost_copy.wait()
    field[shared:both, :] = ghost[...]
    put_shared()
    for copy in copies(0):
        copy.start()

    def vector(value):
        return jnp.full((1, states), value, jnp.float32)

    lowest, cut, upper = vector(bounds[0]), vector(bounds[1]), vector(bounds[2])
    half = (upper - cut) / 2.0
    centre = (upper + cut) / 2.0
    sigma_first = half / (lowest - centre)
    tau = 2.0 / sigma_first

    def degree_step(step, carry):
        alpha, beta, sigma = carry
        slot = lax.rem(step, 2)
        new_rest = (
            matmul(matrix[both:, :], stack[...]) - centre * field[both:, :]
        ) * alpha - beta * before[both:, :]
        before[both:, :] = field[both:, :]
        field[both:, :] = new_rest
        put_rest()
        for copy in copies(slot):
            copy.wait()
        new_shared = (
            outgoing[...] + incoming[slot] - centre * field[0:both, :]
        ) * alpha - beta * before[0:both, :]
        before[0:both, :] = field[0:both, :]
        field[0:both, :] = new_shared
        put_shared()
        for copy in copies(lax.rem(step + 1, 2)):
            copy.start()
        sigma_new = 1.0 / (tau - sigma)
        return 2.0 * sigma_new / half, sigma * sigma_new, sigma_new

    lax.fori_loop(
        0, DEGREE, degree_step, (sigma_first / half, jnp.zeros_like(half), sigma_first)
    )

    result = jnp.concatenate([field[0:shared, :], field[both:, :]], axis=0).T
    filtered[...] = result
    lows[place] = result.astype(jnp.bfloat16)

    def piece_copy(way, hop, piece, block):
        spot = lows.at[block, pl.ds(piece * rows, rows)]
        return pltpu.make_async_remote_copy(
            src_ref=spot,
            dst_ref=spot,
            send_sem=along_send.at[way, hop, piece],
            recv_sem=along_recv.at[way, hop, piece],
            device_id={"state": lax.rem(place + 1 - 2 * way + groups, groups)},
            device_id_type=MESH,
        )

    def block_at(way, hop):
        return lax.rem(place - (1 - 2 * way) * hop + groups, groups)

    def hand_on(way, hop, piece):
        return piece_copy(way, hop, piece, block_at(way, hop))

    def arrival(way, hop, piece):
        return piece_copy(way, hop, piece, block_at(way, hop + 1))

    def sends_at(way, hop):
        if way == 0:
            return jnp.logical_and(place < groups - 1, place >= hop)
        return jnp.logical_and(place > 0, place + hop < groups)

    def receives_at(way, hop):
        if way == 0:
            return place >= hop + 1
        return place + hop + 1 < groups

    for way in range(2):

        @pl.when(sends_at(way, 0))
        def _():
            for piece in range(owners):
                hand_on(way, 0, piece).start()

    image[shared:, :] = matmul(matrix[both:, :], stack[...]).astype(jnp.bfloat16)
    last = DEGREE % 2
    for copy in copies(last):
        copy.wait()
    image[0:shared, :] = (outgoing[0:shared, :] + incoming[last, 0:shared, :]).astype(jnp.bfloat16)

    def swap(block, piece):
        return pltpu.make_async_remote_copy(
            src_ref=parts.at[block, pl.ds(piece * rows, rows)],
            dst_ref=swapped.at[block, pl.ds(piece // 2 * rows, rows)],
            send_sem=swap_send.at[block, piece // 2],
            recv_sem=swap_recv.at[block, piece // 2],
            device_id={"cell": chip * 2 + 1 - core},
            device_id_type=MESH,
        )

    def owner_of(block, piece):
        return block * (owners // 2) + piece // 2

    def shipping(block, piece):
        return pltpu.make_async_remote_copy(
            src_ref=ship.at[block, pl.ds(piece // 2 * rows, rows)],
            dst_ref=gathered.at[chip],
            send_sem=ship_send.at[block, piece // 2],
            recv_sem=ship_recv.at[chip],
            device_id={"cell": 2 * owner_of(block, piece) + core},
            device_id_type=MESH,
        )

    def multiply(block, piece):
        here = slice(piece * rows, (piece + 1) * rows)
        parts[block, here, :] = matmul(lows[block, here, :], image[...])

        @pl.when(core != piece % 2)
        def _():
            swap(block, piece).start()

    def pass_to_owner(block, piece):
        here = slice(piece * rows, (piece + 1) * rows)
        there = slice(piece // 2 * rows, (piece // 2 + 1) * rows)

        @pl.when(core == piece % 2)
        def _():
            swap(block, piece).wait_recv()
            total = parts[block, here, :] + swapped[block, there, :]

            @pl.when(owner_of(block, piece) == chip)
            def _():
                mine[...] = total

            @pl.when(owner_of(block, piece) != chip)
            def _():
                ship[block, there, :] = total
                shipping(block, piece).start()

    for piece in range(owners):
        multiply(place, piece)
    for piece in range(owners):
        pass_to_owner(place, piece)
    for hop in range(groups - 1):
        for piece in range(owners):
            for way in range(2):

                @pl.when(receives_at(way, hop))
                def _():
                    arrival(way, hop, piece).wait_recv()
                    if hop + 1 < groups - 1:

                        @pl.when(sends_at(way, hop + 1))
                        def _():
                            hand_on(way, hop + 1, piece).start()

                    multiply(block_at(way, hop + 1), piece)

            for way in range(2):

                @pl.when(receives_at(way, hop))
                def _():
                    pass_to_owner(block_at(way, hop + 1), piece)

    for way in range(2):
        for hop in range(groups - 1):

            @pl.when(sends_at(way, hop))
            def _():
                for piece in range(owners):
                    hand_on(way, hop, piece).wait_send()

    for block in range(groups):
        for piece in range(owners):

            @pl.when(core != piece % 2)
            def _():
                swap(block, piece).wait_send()

            @pl.when(jnp.logical_and(core == piece % 2, owner_of(block, piece) != chip))
            def _():
                shipping(block, piece).wait_send()

    for other in range(chips):

        @pl.when(other != chip)
        def _():
            pltpu.make_async_remote_copy(
                src_ref=gathered.at[other],
                dst_ref=gathered.at[other],
                send_sem=ship_send.at[0, 0],
                recv_sem=ship_recv.at[other],
                device_id={"cell": 2 * other + core},
                device_id_type=MESH,
            ).wait_recv()
            mine[...] += gathered[other]

    projected[...] = mine[...]


def filtered_block(start, links, cells, bounds, count, groups):
    states, owned = start.shape
    shared = owned // 8
    both = 2 * shared
    extent = owned + shared
    rest = extent - both
    depth = 2 * both + (rest + 127) // 128 * 128 + rest
    rows = states * groups // count
    pairs = states // rows // 2
    chips = count // 2
    vmem = pl.BlockSpec(memory_space=pltpu.VMEM)
    dma = pltpu.SemaphoreType.DMA
    return pl.pallas_call(
        functools.partial(filter_kernel, count, groups),
        out_shape=(
            jax.ShapeDtypeStruct((states, owned), jnp.float32),
            jax.ShapeDtypeStruct((rows, states), jnp.float32),
        ),
        in_specs=[vmem, vmem, vmem, pl.BlockSpec(memory_space=pltpu.SMEM)],
        out_specs=(vmem, vmem),
        scratch_shapes=[
            pltpu.VMEM((extent, depth), jnp.bfloat16),
            pltpu.VMEM((depth, states), jnp.bfloat16),
            pltpu.VMEM((extent, states), jnp.float32),
            pltpu.VMEM((extent, states), jnp.float32),
            pltpu.VMEM((both, states), jnp.float32),
            pltpu.VMEM((both, states), jnp.float32),
            pltpu.VMEM((both, states), jnp.bfloat16),
            pltpu.VMEM((2, both, states), jnp.bfloat16),
            pltpu.VMEM((shared, states), jnp.float32),
            pltpu.VMEM((owned, states), jnp.bfloat16),
            pltpu.VMEM((groups, states, owned), jnp.bfloat16),
            pltpu.VMEM((groups, states, states), jnp.float32),
            pltpu.VMEM((groups, pairs * rows, states), jnp.float32),
            pltpu.VMEM((groups, pairs * rows, states), jnp.float32),
            pltpu.VMEM((chips, rows, states), jnp.float32),
            pltpu.VMEM((rows, states), jnp.float32),
            dma((2,)),
            dma((2, 2)),
            dma((2,)),
            dma((2, groups, 2 * pairs)),
            dma((2, groups, 2 * pairs)),
            dma((groups, pairs)),
            dma((groups, pairs)),
            dma((groups, pairs)),
            dma((chips,)),
        ],
        compiler_params=pltpu.CompilerParams(
            collective_id=0, has_side_effects=True, vmem_limit_bytes=40 * 1024 * 1024
        ),
    )(start, links, cells, bounds)


def solution(mesh):
    in_specs = (P("state", "cell"), P("cell", None), P("cell", None, None), P())
    out_specs = (P("state", "cell"), P("cell", "state"))
    return jax.shard_map(
        functools.partial(
            filtered_block, count=mesh.shape["cell"], groups=mesh.shape["state"]
        ),
        mesh=mesh, in_specs=in_specs, out_specs=out_specs, check_vma=False,
    )
```

```python
import functools

import jax
import jax.numpy as jnp
from jax import lax
from jax.experimental import pallas as pl
from jax.experimental.pallas import tpu as pltpu
from jax.sharding import PartitionSpec as P

DEGREE = 8
MESH = pl.DeviceIdType.MESH


def matmul(left, right):
    return jnp.dot(left, right, preferred_element_type=jnp.float32)


def filter_kernel(
    count, groups, start, links, cells, bounds, filtered, projected,
    matrix, stack, field, before, inner, outgoing, rounded_out, incoming, ghost,
    image, lows, low_ends, parts, swapped, ship, gathered, mine,
    sends, receives, ghost_sems, along_send, along_recv, swap_send, swap_recv,
    ship_send, ship_recv,
):
    states, owned = start.shape
    shared = owned // 8
    both = 2 * shared
    extent = owned + shared
    rest = extent - both
    first = 2 * both
    second = first + (rest + 127) // 128 * 128
    me = lax.axis_index("cell")
    right, left = lax.rem(me + 1, count), lax.rem(me + count - 1, count)

    rows = projected.shape[0]
    owners = states // rows
    chips = count // 2
    chip, core = me // 2, lax.rem(me, 2)
    place = lax.axis_index("state")

    barrier = pltpu.get_barrier_semaphore()

    def greet(target):
        pl.semaphore_signal(barrier, inc=1, device_id=target, device_id_type=MESH)

    greet({"cell": left})
    greet({"cell": right})
    for other in range(chips):

        @pl.when(other != chip)
        def _():
            greet({"cell": 2 * other + core})

    @pl.when(place > 0)
    def _():
        greet({"state": place - 1})

    @pl.when(place < groups - 1)
    def _():
        greet({"state": place + 1})

    field[0:both, :] = start[:, 0:both].T
    stack[0:both, :] = field[0:both, :].astype(jnp.bfloat16)
    beside = jnp.minimum(place, 1) + jnp.minimum(groups - 1 - place, 1)
    pl.semaphore_wait(barrier, 1 + chips + beside)
    ghost_copy = pltpu.make_async_remote_copy(
        src_ref=outgoing.at[pl.ds(0, shared)],
        dst_ref=ghost,
        send_sem=ghost_sems.at[0],
        recv_sem=ghost_sems.at[1],
        device_id={"cell": left},
        device_id_type=MESH,
    )
    outgoing[0:shared, :] = field[0:shared, :]
    ghost_copy.start()

    whole = start[...].T
    field[both:, :] = whole[shared:, :]
    before[...] = jnp.zeros_like(before)

    for cell in range(links.shape[0]):
        link = links[cell : cell + 1, :]
        row = jnp.where(
            link < shared, link, jnp.where(link < owned, link + shared, link - (owned - shared))
        )
        spread = lax.broadcasted_iota(jnp.int32, (extent, links.shape[1]), 0) == row
        spread = jnp.where(spread, 1.0, 0.0).astype(jnp.bfloat16)
        half_way = matmul(spread, cells[cell]).astype(jnp.bfloat16)
        placed = lax.dot_general(
            half_way, spread, (((1,), (1,)), ((), ())), preferred_element_type=jnp.float32
        ).astype(jnp.bfloat16)
        matrix[:, cell * both : (cell + 1) * both] = placed[:, 0:both]
        begin = first if cell == 0 else second
        matrix[:, begin : begin + rest] = placed[:, both:]
    if second > first + rest:
        matrix[:, first + rest : second] = jnp.zeros((extent, second - first - rest), jnp.bfloat16)
        stack[first + rest : second, :] = jnp.zeros((second - first - rest, states), jnp.bfloat16)

    def put_rest():
        rounded = field[both:, :].astype(jnp.bfloat16)
        stack[first : first + rest, :] = rounded
        stack[second : second + rest, :] = rounded
        inner[...] = matmul(matrix[0:both, first:], stack[first:, :])

    def put_shared():
        rounded = field[0:both, :].astype(jnp.bfloat16)
        stack[0:both, :] = rounded
        stack[both:first, :] = rounded
        total = inner[...] + matmul(matrix[0:both, 0:first], stack[0:first, :])
        outgoing[...] = total
        rounded_out[...] = total.astype(jnp.bfloat16)

    def copies(slot):
        to_left = pltpu.make_async_remote_copy(
            src_ref=rounded_out.at[pl.ds(0, shared)],
            dst_ref=incoming.at[slot, pl.ds(shared, shared)],
            send_sem=sends.at[0],
            recv_sem=receives.at[slot, 0],
            device_id={"cell": left},
            device_id_type=MESH,
        )
        to_right = pltpu.make_async_remote_copy(
            src_ref=rounded_out.at[pl.ds(shared, shared)],
            dst_ref=incoming.at[slot, pl.ds(0, shared)],
            send_sem=sends.at[1],
            recv_sem=receives.at[slot, 1],
            device_id={"cell": right},
            device_id_type=MESH,
        )
        return to_left, to_right

    put_rest()
    ghost_copy.wait()
    field[shared:both, :] = ghost[...]
    put_shared()
    for copy in copies(0):
        copy.start()

    def vector(value):
        return jnp.full((1, states), value, jnp.float32)

    lowest, cut, upper = vector(bounds[0]), vector(bounds[1]), vector(bounds[2])
    half = (upper - cut) / 2.0
    centre = (upper + cut) / 2.0
    sigma_first = half / (lowest - centre)
    tau = 2.0 / sigma_first

    def step_rest(alpha, beta):
        new_rest = (
            matmul(matrix[both:, :], stack[...]) - centre * field[both:, :]
        ) * alpha - beta * before[both:, :]
        before[both:, :] = field[both:, :]
        field[both:, :] = new_rest

    def step_shared(step, alpha, beta):
        slot = lax.rem(step, 2)
        for copy in copies(slot):
            copy.wait()
        new_shared = (
            outgoing[...] + incoming[slot] - centre * field[0:both, :]
        ) * alpha - beta * before[0:both, :]
        before[0:both, :] = field[0:both, :]
        field[0:both, :] = new_shared
        put_shared()
        for copy in copies(lax.rem(step + 1, 2)):
            copy.start()

    def degree_step(step, carry):
        alpha, beta, sigma = carry
        step_rest(alpha, beta)
        put_rest()
        step_shared(step, alpha, beta)
        sigma_new = 1.0 / (tau - sigma)
        return 2.0 * sigma_new / half, sigma * sigma_new, sigma_new

    alpha, beta, _ = lax.fori_loop(
        0, DEGREE - 1, degree_step, (sigma_first / half, jnp.zeros_like(half), sigma_first)
    )

    def piece_copy(way, hop, piece, block, part):
        spot = (lows, low_ends)[part].at[block, pl.ds(piece * rows, rows)]
        return pltpu.make_async_remote_copy(
            src_ref=spot,
            dst_ref=spot,
            send_sem=along_send.at[way, hop, piece, part],
            recv_sem=along_recv.at[way, hop, piece, part],
            device_id={"state": lax.rem(place + 1 - 2 * way + groups, groups)},
            device_id_type=MESH,
        )

    def block_at(way, hop):
        return lax.rem(place - (1 - 2 * way) * hop + groups, groups)

    def hand_on(way, hop, piece, part):
        return piece_copy(way, hop, piece, block_at(way, hop), part)

    def arrival(way, hop, piece, part):
        return piece_copy(way, hop, piece, block_at(way, hop + 1), part)

    def sends_at(way, hop):
        if way == 0:
            return jnp.logical_and(place < groups - 1, place >= hop)
        return jnp.logical_and(place > 0, place + hop < groups)

    def receives_at(way, hop):
        if way == 0:
            return place >= hop + 1
        return place + hop + 1 < groups

    def send_own(part):
        for way in range(2):

            @pl.when(sends_at(way, 0))
            def _():
                for piece in range(owners):
                    hand_on(way, 0, piece, part).start()

    early = owned - 128
    step_rest(alpha, beta)
    lows[place] = field[both : both + early, :].T.astype(jnp.bfloat16)
    send_own(0)
    put_rest()
    step_shared(DEGREE - 1, alpha, beta)
    tail = jnp.concatenate([field[both + early :, :], field[0:shared, :]], axis=0)
    low_ends[place] = tail.T.astype(jnp.bfloat16)
    send_own(1)
    image[0:rest, :] = matmul(matrix[both:, :], stack[...]).astype(jnp.bfloat16)
    filtered[...] = jnp.concatenate([field[0:shared, :], field[both:, :]], axis=0).T
    last = DEGREE % 2
    for copy in copies(last):
        copy.wait()
    image[rest:, :] = (outgoing[0:shared, :] + incoming[last, 0:shared, :]).astype(jnp.bfloat16)

    def swap(block, piece):
        return pltpu.make_async_remote_copy(
            src_ref=parts.at[block, pl.ds(piece * rows, rows)],
            dst_ref=swapped.at[block, pl.ds(piece // 2 * rows, rows)],
            send_sem=swap_send.at[block, piece // 2],
            recv_sem=swap_recv.at[block, piece // 2],
            device_id={"cell": chip * 2 + 1 - core},
            device_id_type=MESH,
        )

    def owner_of(block, piece):
        return block * (owners // 2) + piece // 2

    def shipping(block, piece):
        return pltpu.make_async_remote_copy(
            src_ref=ship.at[block, pl.ds(piece // 2 * rows, rows)],
            dst_ref=gathered.at[chip],
            send_sem=ship_send.at[block, piece // 2],
            recv_sem=ship_recv.at[chip],
            device_id={"cell": 2 * owner_of(block, piece) + core},
            device_id_type=MESH,
        )

    def multiply(block, piece):
        here = slice(piece * rows, (piece + 1) * rows)
        parts[block, here, :] = matmul(lows[block, here, :], image[0:early, :]) + matmul(
            low_ends[block, here, :], image[early:, :]
        )

        @pl.when(core != piece % 2)
        def _():
            swap(block, piece).start()

    def pass_to_owner(block, piece):
        here = slice(piece * rows, (piece + 1) * rows)
        there = slice(piece // 2 * rows, (piece // 2 + 1) * rows)

        @pl.when(core == piece % 2)
        def _():
            swap(block, piece).wait_recv()
            total = parts[block, here, :] + swapped[block, there, :]

            @pl.when(owner_of(block, piece) == chip)
            def _():
                mine[...] = total

            @pl.when(owner_of(block, piece) != chip)
            def _():
                ship[block, there, :] = total
                shipping(block, piece).start()

    for piece in range(owners):
        multiply(place, piece)
    for piece in range(owners):
        pass_to_owner(place, piece)
    for hop in range(groups - 1):
        for piece in range(owners):
            for way in range(2):

                @pl.when(receives_at(way, hop))
                def _():
                    for part in range(2):
                        arrival(way, hop, piece, part).wait_recv()
                        if hop + 1 < groups - 1:

                            @pl.when(sends_at(way, hop + 1))
                            def _():
                                hand_on(way, hop + 1, piece, part).start()

                    multiply(block_at(way, hop + 1), piece)

            for way in range(2):

                @pl.when(receives_at(way, hop))
                def _():
                    pass_to_owner(block_at(way, hop + 1), piece)

    for way in range(2):
        for hop in range(groups - 1):

            @pl.when(sends_at(way, hop))
            def _():
                for piece in range(owners):
                    for part in range(2):
                        hand_on(way, hop, piece, part).wait_send()

    for block in range(groups):
        for piece in range(owners):

            @pl.when(core != piece % 2)
            def _():
                swap(block, piece).wait_send()

            @pl.when(jnp.logical_and(core == piece % 2, owner_of(block, piece) != chip))
            def _():
                shipping(block, piece).wait_send()

    for other in range(chips):

        @pl.when(other != chip)
        def _():
            pltpu.make_async_remote_copy(
                src_ref=gathered.at[other],
                dst_ref=gathered.at[other],
                send_sem=ship_send.at[0, 0],
                recv_sem=ship_recv.at[other],
                device_id={"cell": 2 * other + core},
                device_id_type=MESH,
            ).wait_recv()
            mine[...] += gathered[other]

    projected[...] = mine[...]


def filtered_block(start, links, cells, bounds, count, groups):
    states, owned = start.shape
    shared = owned // 8
    both = 2 * shared
    extent = owned + shared
    rest = extent - both
    depth = 2 * both + (rest + 127) // 128 * 128 + rest
    rows = states * groups // count
    pairs = states // rows // 2
    chips = count // 2
    vmem = pl.BlockSpec(memory_space=pltpu.VMEM)
    dma = pltpu.SemaphoreType.DMA
    return pl.pallas_call(
        functools.partial(filter_kernel, count, groups),
        out_shape=(
            jax.ShapeDtypeStruct((states, owned), jnp.float32),
            jax.ShapeDtypeStruct((rows, states), jnp.float32),
        ),
        in_specs=[vmem, vmem, vmem, pl.BlockSpec(memory_space=pltpu.SMEM)],
        out_specs=(vmem, vmem),
        scratch_shapes=[
            pltpu.VMEM((extent, depth), jnp.bfloat16),
            pltpu.VMEM((depth, states), jnp.bfloat16),
            pltpu.VMEM((extent, states), jnp.float32),
            pltpu.VMEM((extent, states), jnp.float32),
            pltpu.VMEM((both, states), jnp.float32),
            pltpu.VMEM((both, states), jnp.float32),
            pltpu.VMEM((both, states), jnp.bfloat16),
            pltpu.VMEM((2, both, states), jnp.bfloat16),
            pltpu.VMEM((shared, states), jnp.float32),
            pltpu.VMEM((owned, states), jnp.bfloat16),
            pltpu.VMEM((groups, states, owned - 128), jnp.bfloat16),
            pltpu.VMEM((groups, states, 128), jnp.bfloat16),
            pltpu.VMEM((groups, states, states), jnp.float32),
            pltpu.VMEM((groups, pairs * rows, states), jnp.float32),
            pltpu.VMEM((groups, pairs * rows, states), jnp.float32),
            pltpu.VMEM((chips, rows, states), jnp.float32),
            pltpu.VMEM((rows, states), jnp.float32),
            dma((2,)),
            dma((2, 2)),
            dma((2,)),
            dma((2, groups, 2 * pairs, 2)),
            dma((2, groups, 2 * pairs, 2)),
            dma((groups, pairs)),
            dma((groups, pairs)),
            dma((groups, pairs)),
            dma((chips,)),
        ],
        compiler_params=pltpu.CompilerParams(
            collective_id=0, has_side_effects=True, vmem_limit_bytes=40 * 1024 * 1024
        ),
    )(start, links, cells, bounds)


def solution(mesh):
    in_specs = (P("state", "cell"), P("cell", None), P("cell", None, None), P())
    out_specs = (P("state", "cell"), P("cell", "state"))
    return jax.shard_map(
        functools.partial(
            filtered_block, count=mesh.shape["cell"], groups=mesh.shape["state"]
        ),
        mesh=mesh, in_specs=in_specs, out_specs=out_specs, check_vma=False,
    )
```

```python
import functools

import jax
import jax.numpy as jnp
from jax import lax
from jax.experimental import pallas as pl
from jax.experimental.pallas import tpu as pltpu
from jax.sharding import PartitionSpec as P

DEGREE = 8
MESH = pl.DeviceIdType.MESH


def matmul(left, right):
    return jnp.dot(left, right, preferred_element_type=jnp.float32)


def filter_kernel(
    count, groups, start, links, cells, bounds, filtered, projected,
    matrix, stack, field, before, inner, outgoing, rounded_out, incoming, ghost,
    image, lows, low_ends, parts, swapped, ship, gathered, mine,
    sends, receives, ghost_sems, along_send, along_recv, swap_send, swap_recv,
    ship_send, ship_recv,
):
    states, owned = start.shape
    shared = owned // 8
    both = 2 * shared
    extent = owned + shared
    rest = extent - both
    first = 2 * both
    second = first + (rest + 127) // 128 * 128
    me = lax.axis_index("cell")
    right, left = lax.rem(me + 1, count), lax.rem(me + count - 1, count)

    rows = projected.shape[0]
    owners = states // rows
    chips = count // 2
    chip, core = me // 2, lax.rem(me, 2)
    place = lax.axis_index("state")

    barrier = pltpu.get_barrier_semaphore()

    def greet(target):
        pl.semaphore_signal(barrier, inc=1, device_id=target, device_id_type=MESH)

    greet({"cell": left})
    greet({"cell": right})
    for other in range(chips):

        @pl.when(other != chip)
        def _():
            greet({"cell": 2 * other + core})

    @pl.when(place > 0)
    def _():
        greet({"state": place - 1})

    @pl.when(place < groups - 1)
    def _():
        greet({"state": place + 1})

    field[0:both, :] = start[:, 0:both].T
    stack[0:both, :] = field[0:both, :].astype(jnp.bfloat16)
    beside = jnp.minimum(place, 1) + jnp.minimum(groups - 1 - place, 1)
    pl.semaphore_wait(barrier, 1 + chips + beside)
    ghost_copy = pltpu.make_async_remote_copy(
        src_ref=outgoing.at[pl.ds(0, shared)],
        dst_ref=ghost,
        send_sem=ghost_sems.at[0],
        recv_sem=ghost_sems.at[1],
        device_id={"cell": left},
        device_id_type=MESH,
    )
    outgoing[0:shared, :] = field[0:shared, :]
    ghost_copy.start()

    whole = start[...].T
    field[both:, :] = whole[shared:, :]
    before[...] = jnp.zeros_like(before)

    for cell in range(links.shape[0]):
        link = links[cell : cell + 1, :]
        row = jnp.where(
            link < shared, link, jnp.where(link < owned, link + shared, link - (owned - shared))
        )
        spread = lax.broadcasted_iota(jnp.int32, (extent, links.shape[1]), 0) == row
        spread = jnp.where(spread, 1.0, 0.0).astype(jnp.bfloat16)
        half_way = matmul(spread, cells[cell]).astype(jnp.bfloat16)
        placed = lax.dot_general(
            half_way, spread, (((1,), (1,)), ((), ())), preferred_element_type=jnp.float32
        ).astype(jnp.bfloat16)
        matrix[:, cell * both : (cell + 1) * both] = placed[:, 0:both]
        begin = first if cell == 0 else second
        matrix[:, begin : begin + rest] = placed[:, both:]
    if second > first + rest:
        matrix[:, first + rest : second] = jnp.zeros((extent, second - first - rest), jnp.bfloat16)
        stack[first + rest : second, :] = jnp.zeros((second - first - rest, states), jnp.bfloat16)

    def put_rest():
        rounded = field[both:, :].astype(jnp.bfloat16)
        stack[first : first + rest, :] = rounded
        stack[second : second + rest, :] = rounded
        inner[...] = matmul(matrix[0:both, first:], stack[first:, :])

    def put_shared():
        rounded = field[0:both, :].astype(jnp.bfloat16)
        stack[0:both, :] = rounded
        stack[both:first, :] = rounded
        total = inner[...] + matmul(matrix[0:both, 0:first], stack[0:first, :])
        outgoing[...] = total
        rounded_out[...] = total.astype(jnp.bfloat16)

    def copies(slot):
        to_left = pltpu.make_async_remote_copy(
            src_ref=rounded_out.at[pl.ds(0, shared)],
            dst_ref=incoming.at[slot, pl.ds(shared, shared)],
            send_sem=sends.at[0],
            recv_sem=receives.at[slot, 0],
            device_id={"cell": left},
            device_id_type=MESH,
        )
        to_right = pltpu.make_async_remote_copy(
            src_ref=rounded_out.at[pl.ds(shared, shared)],
            dst_ref=incoming.at[slot, pl.ds(0, shared)],
            send_sem=sends.at[1],
            recv_sem=receives.at[slot, 1],
            device_id={"cell": right},
            device_id_type=MESH,
        )
        return to_left, to_right

    put_rest()
    ghost_copy.wait()
    field[shared:both, :] = ghost[...]
    put_shared()
    for copy in copies(0):
        copy.start()

    def vector(value):
        return jnp.full((1, states), value, jnp.float32)

    lowest, cut, upper = vector(bounds[0]), vector(bounds[1]), vector(bounds[2])
    half = (upper - cut) / 2.0
    centre = (upper + cut) / 2.0
    sigma_first = half / (lowest - centre)
    tau = 2.0 / sigma_first

    def step_rest(alpha, beta):
        new_rest = (
            matmul(matrix[both:, :], stack[...]) - centre * field[both:, :]
        ) * alpha - beta * before[both:, :]
        before[both:, :] = field[both:, :]
        field[both:, :] = new_rest

    def step_shared(step, alpha, beta):
        slot = lax.rem(step, 2)
        for copy in copies(slot):
            copy.wait()
        new_shared = (
            outgoing[...] + incoming[slot] - centre * field[0:both, :]
        ) * alpha - beta * before[0:both, :]
        before[0:both, :] = field[0:both, :]
        field[0:both, :] = new_shared
        put_shared()
        for copy in copies(lax.rem(step + 1, 2)):
            copy.start()

    def degree_step(step, carry):
        alpha, beta, sigma = carry
        step_rest(alpha, beta)
        put_rest()
        step_shared(step, alpha, beta)
        sigma_new = 1.0 / (tau - sigma)
        return 2.0 * sigma_new / half, sigma * sigma_new, sigma_new

    alpha, beta, _ = lax.fori_loop(
        0, DEGREE - 1, degree_step, (sigma_first / half, jnp.zeros_like(half), sigma_first)
    )

    def piece_copy(way, hop, piece, block, part):
        spot = (lows, low_ends)[part].at[block, pl.ds(piece * rows, rows)]
        return pltpu.make_async_remote_copy(
            src_ref=spot,
            dst_ref=spot,
            send_sem=along_send.at[way, hop, piece, part],
            recv_sem=along_recv.at[way, hop, piece, part],
            device_id={"state": lax.rem(place + 1 - 2 * way + groups, groups)},
            device_id_type=MESH,
        )

    def block_at(way, hop):
        return lax.rem(place - (1 - 2 * way) * hop + groups, groups)

    def hand_on(way, hop, piece, part):
        return piece_copy(way, hop, piece, block_at(way, hop), part)

    def arrival(way, hop, piece, part):
        return piece_copy(way, hop, piece, block_at(way, hop + 1), part)

    def sends_at(way, hop):
        if way == 0:
            return jnp.logical_and(place < groups - 1, place >= hop)
        return jnp.logical_and(place > 0, place + hop < groups)

    def receives_at(way, hop):
        if way == 0:
            return place >= hop + 1
        return place + hop + 1 < groups

    def send_own(part):
        for way in range(2):

            @pl.when(sends_at(way, 0))
            def _():
                for piece in range(owners):
                    hand_on(way, 0, piece, part).start()

    early = owned - 128
    step_rest(alpha, beta)
    lows[place] = field[both : both + early, :].T.astype(jnp.bfloat16)
    send_own(0)
    put_rest()
    step_shared(DEGREE - 1, alpha, beta)
    tail = jnp.concatenate([field[both + early :, :], field[0:shared, :]], axis=0)
    low_ends[place] = tail.T.astype(jnp.bfloat16)
    send_own(1)
    image[0:rest, :] = matmul(matrix[both:, :], stack[...]).astype(jnp.bfloat16)
    filtered[...] = jnp.concatenate([field[0:shared, :], field[both:, :]], axis=0).T
    last = DEGREE % 2
    for copy in copies(last):
        copy.wait()
    image[rest:, :] = (outgoing[0:shared, :] + incoming[last, 0:shared, :]).astype(jnp.bfloat16)

    def swap(block, piece):
        return pltpu.make_async_remote_copy(
            src_ref=parts.at[block, pl.ds(piece * rows, rows)],
            dst_ref=swapped.at[block, pl.ds(piece // 2 * rows, rows)],
            send_sem=swap_send.at[block, piece // 2],
            recv_sem=swap_recv.at[block, piece // 2],
            device_id={"cell": chip * 2 + 1 - core},
            device_id_type=MESH,
        )

    def owner_of(block, piece):
        return block * (owners // 2) + piece // 2

    def shipping(block, piece):
        return pltpu.make_async_remote_copy(
            src_ref=ship.at[block, pl.ds(piece // 2 * rows, rows)],
            dst_ref=gathered.at[chip],
            send_sem=ship_send.at[block, piece // 2],
            recv_sem=ship_recv.at[chip],
            device_id={"cell": 2 * owner_of(block, piece) + core},
            device_id_type=MESH,
        )

    def multiply(block, piece):
        here = slice(piece * rows, (piece + 1) * rows)
        parts[block, here, :] = matmul(lows[block, here, :], image[0:early, :]) + matmul(
            low_ends[block, here, :], image[early:, :]
        )

        @pl.when(core != piece % 2)
        def _():
            swap(block, piece).start()

    def pass_to_owner(block, piece):
        here = slice(piece * rows, (piece + 1) * rows)
        there = slice(piece // 2 * rows, (piece // 2 + 1) * rows)

        @pl.when(core == piece % 2)
        def _():
            swap(block, piece).wait_recv()
            total = parts[block, here, :] + swapped[block, there, :]

            @pl.when(owner_of(block, piece) == chip)
            def _():
                mine[...] = total

            @pl.when(owner_of(block, piece) != chip)
            def _():
                ship[block, there, :] = total
                shipping(block, piece).start()

    def pass_own():
        for piece in range(owners):
            pass_to_owner(place, piece)

    def pass_arrived(hop, piece):
        for way in range(2):

            @pl.when(receives_at(way, hop))
            def _():
                pass_to_owner(block_at(way, hop + 1), piece)

    for piece in range(owners):
        multiply(place, piece)
    waiting = [pass_own]
    for hop in range(groups - 1):
        for piece in range(owners):
            for way in range(2):

                @pl.when(receives_at(way, hop))
                def _():
                    for part in range(2):
                        arrival(way, hop, piece, part).wait_recv()
                        if hop + 1 < groups - 1:

                            @pl.when(sends_at(way, hop + 1))
                            def _():
                                hand_on(way, hop + 1, piece, part).start()

                    multiply(block_at(way, hop + 1), piece)

            for pending in waiting:
                pending()
            waiting = [functools.partial(pass_arrived, hop, piece)]
            if hop == groups - 2:
                waiting.pop()()
    for pending in waiting:
        pending()

    for way in range(2):
        for hop in range(groups - 1):

            @pl.when(sends_at(way, hop))
            def _():
                for piece in range(owners):
                    for part in range(2):
                        hand_on(way, hop, piece, part).wait_send()

    for block in range(groups):
        for piece in range(owners):

            @pl.when(core != piece % 2)
            def _():
                swap(block, piece).wait_send()

            @pl.when(jnp.logical_and(core == piece % 2, owner_of(block, piece) != chip))
            def _():
                shipping(block, piece).wait_send()

    for other in range(chips):

        @pl.when(other != chip)
        def _():
            pltpu.make_async_remote_copy(
                src_ref=gathered.at[other],
                dst_ref=gathered.at[other],
                send_sem=ship_send.at[0, 0],
                recv_sem=ship_recv.at[other],
                device_id={"cell": 2 * other + core},
                device_id_type=MESH,
            ).wait_recv()
            mine[...] += gathered[other]

    projected[...] = mine[...]


def filtered_block(start, links, cells, bounds, count, groups):
    states, owned = start.shape
    shared = owned // 8
    both = 2 * shared
    extent = owned + shared
    rest = extent - both
    depth = 2 * both + (rest + 127) // 128 * 128 + rest
    rows = states * groups // count
    pairs = states // rows // 2
    chips = count // 2
    vmem = pl.BlockSpec(memory_space=pltpu.VMEM)
    dma = pltpu.SemaphoreType.DMA
    return pl.pallas_call(
        functools.partial(filter_kernel, count, groups),
        out_shape=(
            jax.ShapeDtypeStruct((states, owned), jnp.float32),
            jax.ShapeDtypeStruct((rows, states), jnp.float32),
        ),
        in_specs=[vmem, vmem, vmem, pl.BlockSpec(memory_space=pltpu.SMEM)],
        out_specs=(vmem, vmem),
        scratch_shapes=[
            pltpu.VMEM((extent, depth), jnp.bfloat16),
            pltpu.VMEM((depth, states), jnp.bfloat16),
            pltpu.VMEM((extent, states), jnp.float32),
            pltpu.VMEM((extent, states), jnp.float32),
            pltpu.VMEM((both, states), jnp.float32),
            pltpu.VMEM((both, states), jnp.float32),
            pltpu.VMEM((both, states), jnp.bfloat16),
            pltpu.VMEM((2, both, states), jnp.bfloat16),
            pltpu.VMEM((shared, states), jnp.float32),
            pltpu.VMEM((owned, states), jnp.bfloat16),
            pltpu.VMEM((groups, states, owned - 128), jnp.bfloat16),
            pltpu.VMEM((groups, states, 128), jnp.bfloat16),
            pltpu.VMEM((groups, states, states), jnp.float32),
            pltpu.VMEM((groups, pairs * rows, states), jnp.float32),
            pltpu.VMEM((groups, pairs * rows, states), jnp.float32),
            pltpu.VMEM((chips, rows, states), jnp.float32),
            pltpu.VMEM((rows, states), jnp.float32),
            dma((2,)),
            dma((2, 2)),
            dma((2,)),
            dma((2, groups, 2 * pairs, 2)),
            dma((2, groups, 2 * pairs, 2)),
            dma((groups, pairs)),
            dma((groups, pairs)),
            dma((groups, pairs)),
            dma((chips,)),
        ],
        compiler_params=pltpu.CompilerParams(
            collective_id=0, has_side_effects=True, vmem_limit_bytes=40 * 1024 * 1024
        ),
    )(start, links, cells, bounds)


def solution(mesh):
    in_specs = (P("state", "cell"), P("cell", None), P("cell", None, None), P())
    out_specs = (P("state", "cell"), P("cell", "state"))
    return jax.shard_map(
        functools.partial(
            filtered_block, count=mesh.shape["cell"], groups=mesh.shape["state"]
        ),
        mesh=mesh, in_specs=in_specs, out_specs=out_specs, check_vma=False,
    )
```

```python
import functools

import jax
import jax.numpy as jnp
from jax import lax
from jax.experimental import pallas as pl
from jax.experimental.pallas import tpu as pltpu
from jax.sharding import PartitionSpec as P

DEGREE = 8
MESH = pl.DeviceIdType.MESH


def matmul(left, right):
    return jnp.dot(left, right, preferred_element_type=jnp.float32)


def filter_kernel(
    count, groups, start, links, cells, bounds, filtered, projected,
    matrix, stack, field, before, inner, outgoing, rounded_out, incoming, ghost,
    image, lows, low_ends, parts, swapped, ship, gathered, mine,
    sends, receives, ghost_sems, along_send, along_recv, swap_send, swap_recv,
    ship_send, ship_recv,
):
    states, owned = start.shape
    shared = owned // 8
    both = 2 * shared
    extent = owned + shared
    rest = extent - both
    first = 2 * both
    second = first + (rest + 127) // 128 * 128
    me = lax.axis_index("cell")
    right, left = lax.rem(me + 1, count), lax.rem(me + count - 1, count)

    rows = projected.shape[0]
    owners = states // rows
    chips = count // 2
    chip, core = me // 2, lax.rem(me, 2)
    place = lax.axis_index("state")

    barrier = pltpu.get_barrier_semaphore()

    def greet(target):
        pl.semaphore_signal(barrier, inc=1, device_id=target, device_id_type=MESH)

    greet({"cell": left})
    greet({"cell": right})
    for other in range(chips):

        @pl.when(other != chip)
        def _():
            greet({"cell": 2 * other + core})

    @pl.when(place > 0)
    def _():
        greet({"state": place - 1})

    @pl.when(place < groups - 1)
    def _():
        greet({"state": place + 1})

    field[0:both, :] = start[:, 0:both].T
    stack[0:both, :] = field[0:both, :].astype(jnp.bfloat16)
    ghost_copy = pltpu.make_async_remote_copy(
        src_ref=outgoing.at[pl.ds(0, shared)],
        dst_ref=ghost,
        send_sem=ghost_sems.at[0],
        recv_sem=ghost_sems.at[1],
        device_id={"cell": left},
        device_id_type=MESH,
    )
    outgoing[0:shared, :] = field[0:shared, :]

    whole = start[...].T
    field[both:, :] = whole[shared:, :]
    before[...] = jnp.zeros_like(before)

    for cell in range(links.shape[0]):
        link = links[cell : cell + 1, :]
        row = jnp.where(
            link < shared, link, jnp.where(link < owned, link + shared, link - (owned - shared))
        )
        spread = lax.broadcasted_iota(jnp.int32, (extent, links.shape[1]), 0) == row
        spread = jnp.where(spread, 1.0, 0.0).astype(jnp.bfloat16)
        half_way = matmul(spread, cells[cell]).astype(jnp.bfloat16)
        placed = lax.dot_general(
            half_way, spread, (((1,), (1,)), ((), ())), preferred_element_type=jnp.float32
        ).astype(jnp.bfloat16)
        matrix[:, cell * both : (cell + 1) * both] = placed[:, 0:both]
        begin = first if cell == 0 else second
        matrix[:, begin : begin + rest] = placed[:, both:]
        if cell == 0:
            beside = jnp.minimum(place, 1) + jnp.minimum(groups - 1 - place, 1)
            pl.semaphore_wait(barrier, 1 + chips + beside)
            ghost_copy.start()
    if second > first + rest:
        matrix[:, first + rest : second] = jnp.zeros((extent, second - first - rest), jnp.bfloat16)
        stack[first + rest : second, :] = jnp.zeros((second - first - rest, states), jnp.bfloat16)

    def put_rest():
        rounded = field[both:, :].astype(jnp.bfloat16)
        stack[first : first + rest, :] = rounded
        stack[second : second + rest, :] = rounded
        inner[...] = matmul(matrix[0:both, first:], stack[first:, :])

    def put_shared():
        rounded = field[0:both, :].astype(jnp.bfloat16)
        stack[0:both, :] = rounded
        stack[both:first, :] = rounded
        total = inner[...] + matmul(matrix[0:both, 0:first], stack[0:first, :])
        outgoing[...] = total
        rounded_out[...] = total.astype(jnp.bfloat16)

    def copies(slot):
        to_left = pltpu.make_async_remote_copy(
            src_ref=rounded_out.at[pl.ds(0, shared)],
            dst_ref=incoming.at[slot, pl.ds(shared, shared)],
            send_sem=sends.at[0],
            recv_sem=receives.at[slot, 0],
            device_id={"cell": left},
            device_id_type=MESH,
        )
        to_right = pltpu.make_async_remote_copy(
            src_ref=rounded_out.at[pl.ds(shared, shared)],
            dst_ref=incoming.at[slot, pl.ds(0, shared)],
            send_sem=sends.at[1],
            recv_sem=receives.at[slot, 1],
            device_id={"cell": right},
            device_id_type=MESH,
        )
        return to_left, to_right

    put_rest()
    ghost_copy.wait()
    field[shared:both, :] = ghost[...]
    put_shared()
    for copy in copies(0):
        copy.start()

    def vector(value):
        return jnp.full((1, states), value, jnp.float32)

    lowest, cut, upper = vector(bounds[0]), vector(bounds[1]), vector(bounds[2])
    half = (upper - cut) / 2.0
    centre = (upper + cut) / 2.0
    sigma_first = half / (lowest - centre)
    tau = 2.0 / sigma_first

    def step_rest(alpha, beta):
        new_rest = (
            matmul(matrix[both:, :], stack[...]) - centre * field[both:, :]
        ) * alpha - beta * before[both:, :]
        before[both:, :] = field[both:, :]
        field[both:, :] = new_rest

    def step_shared(step, alpha, beta):
        slot = lax.rem(step, 2)
        for copy in copies(slot):
            copy.wait()
        new_shared = (
            outgoing[...] + incoming[slot] - centre * field[0:both, :]
        ) * alpha - beta * before[0:both, :]
        before[0:both, :] = field[0:both, :]
        field[0:both, :] = new_shared
        put_shared()
        for copy in copies(lax.rem(step + 1, 2)):
            copy.start()

    def degree_step(step, carry):
        alpha, beta, sigma = carry
        step_rest(alpha, beta)
        put_rest()
        step_shared(step, alpha, beta)
        sigma_new = 1.0 / (tau - sigma)
        return 2.0 * sigma_new / half, sigma * sigma_new, sigma_new

    alpha, beta, _ = lax.fori_loop(
        0, DEGREE - 1, degree_step, (sigma_first / half, jnp.zeros_like(half), sigma_first)
    )

    def piece_copy(way, hop, piece, block, part):
        spot = (lows, low_ends)[part].at[block, pl.ds(piece * rows, rows)]
        return pltpu.make_async_remote_copy(
            src_ref=spot,
            dst_ref=spot,
            send_sem=along_send.at[way, hop, piece, part],
            recv_sem=along_recv.at[way, hop, piece, part],
            device_id={"state": lax.rem(place + 1 - 2 * way + groups, groups)},
            device_id_type=MESH,
        )

    def block_at(way, hop):
        return lax.rem(place - (1 - 2 * way) * hop + groups, groups)

    def hand_on(way, hop, piece, part):
        return piece_copy(way, hop, piece, block_at(way, hop), part)

    def arrival(way, hop, piece, part):
        return piece_copy(way, hop, piece, block_at(way, hop + 1), part)

    def sends_at(way, hop):
        if way == 0:
            return jnp.logical_and(place < groups - 1, place >= hop)
        return jnp.logical_and(place > 0, place + hop < groups)

    def receives_at(way, hop):
        if way == 0:
            return place >= hop + 1
        return place + hop + 1 < groups

    def send_own(part):
        for way in range(2):

            @pl.when(sends_at(way, 0))
            def _():
                for piece in range(owners):
                    hand_on(way, 0, piece, part).start()

    early = owned - 128
    step_rest(alpha, beta)
    lows[place] = field[both : both + early, :].T.astype(jnp.bfloat16)
    send_own(0)
    put_rest()
    step_shared(DEGREE - 1, alpha, beta)
    tail = jnp.concatenate([field[both + early :, :], field[0:shared, :]], axis=0)
    low_ends[place] = tail.T.astype(jnp.bfloat16)
    send_own(1)
    image[0:rest, :] = matmul(matrix[both:, :], stack[...]).astype(jnp.bfloat16)
    filtered[...] = jnp.concatenate([field[0:shared, :], field[both:, :]], axis=0).T
    last = DEGREE % 2
    for copy in copies(last):
        copy.wait()
    image[rest:, :] = (outgoing[0:shared, :] + incoming[last, 0:shared, :]).astype(jnp.bfloat16)

    def swap(block, piece):
        return pltpu.make_async_remote_copy(
            src_ref=parts.at[block, pl.ds(piece * rows, rows)],
            dst_ref=swapped.at[block, pl.ds(piece // 2 * rows, rows)],
            send_sem=swap_send.at[block, piece // 2],
            recv_sem=swap_recv.at[block, piece // 2],
            device_id={"cell": chip * 2 + 1 - core},
            device_id_type=MESH,
        )

    def owner_of(block, piece):
        return block * (owners // 2) + piece // 2

    def shipping(block, piece):
        return pltpu.make_async_remote_copy(
            src_ref=ship.at[block, pl.ds(piece // 2 * rows, rows)],
            dst_ref=gathered.at[chip],
            send_sem=ship_send.at[block, piece // 2],
            recv_sem=ship_recv.at[chip],
            device_id={"cell": 2 * owner_of(block, piece) + core},
            device_id_type=MESH,
        )

    def multiply(block, piece):
        here = slice(piece * rows, (piece + 1) * rows)
        parts[block, here, :] = matmul(lows[block, here, :], image[0:early, :]) + matmul(
            low_ends[block, here, :], image[early:, :]
        )

        @pl.when(core != piece % 2)
        def _():
            swap(block, piece).start()

    def pass_to_owner(block, piece):
        here = slice(piece * rows, (piece + 1) * rows)
        there = slice(piece // 2 * rows, (piece // 2 + 1) * rows)

        @pl.when(core == piece % 2)
        def _():
            swap(block, piece).wait_recv()
            total = parts[block, here, :] + swapped[block, there, :]

            @pl.when(owner_of(block, piece) == chip)
            def _():
                mine[...] = total

            @pl.when(owner_of(block, piece) != chip)
            def _():
                ship[block, there, :] = total
                shipping(block, piece).start()

    def pass_own():
        for piece in range(owners):
            pass_to_owner(place, piece)

    def pass_arrived(hop, piece):
        for way in range(2):

            @pl.when(receives_at(way, hop))
            def _():
                pass_to_owner(block_at(way, hop + 1), piece)

    for piece in range(owners):
        multiply(place, piece)
    waiting = [pass_own]
    for hop in range(groups - 1):
        for piece in range(owners):
            for way in range(2):

                @pl.when(receives_at(way, hop))
                def _():
                    for part in range(2):
                        arrival(way, hop, piece, part).wait_recv()
                        if hop + 1 < groups - 1:

                            @pl.when(sends_at(way, hop + 1))
                            def _():
                                hand_on(way, hop + 1, piece, part).start()

                    multiply(block_at(way, hop + 1), piece)

            for pending in waiting:
                pending()
            waiting = [functools.partial(pass_arrived, hop, piece)]
            if hop == groups - 2:
                waiting.pop()()
    for pending in waiting:
        pending()

    for way in range(2):
        for hop in range(groups - 1):

            @pl.when(sends_at(way, hop))
            def _():
                for piece in range(owners):
                    for part in range(2):
                        hand_on(way, hop, piece, part).wait_send()

    for block in range(groups):
        for piece in range(owners):

            @pl.when(core != piece % 2)
            def _():
                swap(block, piece).wait_send()

            @pl.when(jnp.logical_and(core == piece % 2, owner_of(block, piece) != chip))
            def _():
                shipping(block, piece).wait_send()

    for other in range(chips):

        @pl.when(other != chip)
        def _():
            pltpu.make_async_remote_copy(
                src_ref=gathered.at[other],
                dst_ref=gathered.at[other],
                send_sem=ship_send.at[0, 0],
                recv_sem=ship_recv.at[other],
                device_id={"cell": 2 * other + core},
                device_id_type=MESH,
            ).wait_recv()
            mine[...] += gathered[other]

    projected[...] = mine[...]


def filtered_block(start, links, cells, bounds, count, groups):
    states, owned = start.shape
    shared = owned // 8
    both = 2 * shared
    extent = owned + shared
    rest = extent - both
    depth = 2 * both + (rest + 127) // 128 * 128 + rest
    rows = states * groups // count
    pairs = states // rows // 2
    chips = count // 2
    vmem = pl.BlockSpec(memory_space=pltpu.VMEM)
    dma = pltpu.SemaphoreType.DMA
    return pl.pallas_call(
        functools.partial(filter_kernel, count, groups),
        out_shape=(
            jax.ShapeDtypeStruct((states, owned), jnp.float32),
            jax.ShapeDtypeStruct((rows, states), jnp.float32),
        ),
        in_specs=[vmem, vmem, vmem, pl.BlockSpec(memory_space=pltpu.SMEM)],
        out_specs=(vmem, vmem),
        scratch_shapes=[
            pltpu.VMEM((extent, depth), jnp.bfloat16),
            pltpu.VMEM((depth, states), jnp.bfloat16),
            pltpu.VMEM((extent, states), jnp.float32),
            pltpu.VMEM((extent, states), jnp.float32),
            pltpu.VMEM((both, states), jnp.float32),
            pltpu.VMEM((both, states), jnp.float32),
            pltpu.VMEM((both, states), jnp.bfloat16),
            pltpu.VMEM((2, both, states), jnp.bfloat16),
            pltpu.VMEM((shared, states), jnp.float32),
            pltpu.VMEM((owned, states), jnp.bfloat16),
            pltpu.VMEM((groups, states, owned - 128), jnp.bfloat16),
            pltpu.VMEM((groups, states, 128), jnp.bfloat16),
            pltpu.VMEM((groups, states, states), jnp.float32),
            pltpu.VMEM((groups, pairs * rows, states), jnp.float32),
            pltpu.VMEM((groups, pairs * rows, states), jnp.float32),
            pltpu.VMEM((chips, rows, states), jnp.float32),
            pltpu.VMEM((rows, states), jnp.float32),
            dma((2,)),
            dma((2, 2)),
            dma((2,)),
            dma((2, groups, 2 * pairs, 2)),
            dma((2, groups, 2 * pairs, 2)),
            dma((groups, pairs)),
            dma((groups, pairs)),
            dma((groups, pairs)),
            dma((chips,)),
        ],
        compiler_params=pltpu.CompilerParams(
            collective_id=0, has_side_effects=True, vmem_limit_bytes=40 * 1024 * 1024
        ),
    )(start, links, cells, bounds)


def solution(mesh):
    in_specs = (P("state", "cell"), P("cell", None), P("cell", None, None), P())
    out_specs = (P("state", "cell"), P("cell", "state"))
    return jax.shard_map(
        functools.partial(
            filtered_block, count=mesh.shape["cell"], groups=mesh.shape["state"]
        ),
        mesh=mesh, in_specs=in_specs, out_specs=out_specs, check_vma=False,
    )
```

```python
import functools

import jax
import jax.numpy as jnp
from jax import lax
from jax.experimental import pallas as pl
from jax.experimental.pallas import tpu as pltpu
from jax.sharding import PartitionSpec as P

DEGREE = 8
MESH = pl.DeviceIdType.MESH


def matmul(left, right):
    return jnp.dot(left, right, preferred_element_type=jnp.float32)


def filter_kernel(
    count, groups, start, links, cells, bounds, filtered, projected,
    matrix, stack, field, before, inner, outgoing, rounded_out, incoming, ghost,
    image, lows, low_ends, parts, swapped, ship, gathered, mine,
    sends, receives, ghost_sems, along_send, along_recv, swap_send, swap_recv,
    ship_send, ship_recv,
):
    states, owned = start.shape
    shared = owned // 8
    both = 2 * shared
    extent = owned + shared
    rest = extent - both
    first = 2 * both
    second = first + (rest + 127) // 128 * 128
    me = lax.axis_index("cell")
    right, left = lax.rem(me + 1, count), lax.rem(me + count - 1, count)

    rows = projected.shape[0]
    owners = states // rows
    chips = count // 2
    chip, core = me // 2, lax.rem(me, 2)
    place = lax.axis_index("state")

    barrier = pltpu.get_barrier_semaphore()

    def greet(target):
        pl.semaphore_signal(barrier, inc=1, device_id=target, device_id_type=MESH)

    greet({"cell": left})
    greet({"cell": right})
    for other in range(chips):

        @pl.when(other != chip)
        def _():
            greet({"cell": 2 * other + core})

    @pl.when(place > 0)
    def _():
        greet({"state": place - 1})

    @pl.when(place < groups - 1)
    def _():
        greet({"state": place + 1})

    field[0:both, :] = start[:, 0:both].T
    stack[0:both, :] = field[0:both, :].astype(jnp.bfloat16)
    ghost_copy = pltpu.make_async_remote_copy(
        src_ref=outgoing.at[pl.ds(0, shared)],
        dst_ref=ghost,
        send_sem=ghost_sems.at[0],
        recv_sem=ghost_sems.at[1],
        device_id={"cell": left},
        device_id_type=MESH,
    )
    outgoing[0:shared, :] = field[0:shared, :]

    whole = start[...].T
    field[both:, :] = whole[shared:, :]
    before[...] = jnp.zeros_like(before)

    for cell in range(links.shape[0]):
        link = links[cell : cell + 1, :]
        row = jnp.where(
            link < shared, link, jnp.where(link < owned, link + shared, link - (owned - shared))
        )
        spread = lax.broadcasted_iota(jnp.int32, (extent, links.shape[1]), 0) == row
        spread = jnp.where(spread, 1.0, 0.0).astype(jnp.bfloat16)
        half_way = matmul(spread, cells[cell]).astype(jnp.bfloat16)
        placed = lax.dot_general(
            half_way, spread, (((1,), (1,)), ((), ())), preferred_element_type=jnp.float32
        ).astype(jnp.bfloat16)
        matrix[:, cell * both : (cell + 1) * both] = placed[:, 0:both]
        begin = first if cell == 0 else second
        matrix[:, begin : begin + rest] = placed[:, both:]
        if cell == 0:
            beside = jnp.minimum(place, 1) + jnp.minimum(groups - 1 - place, 1)
            pl.semaphore_wait(barrier, 1 + chips + beside)
            ghost_copy.start()
    if second > first + rest:
        matrix[:, first + rest : second] = jnp.zeros((extent, second - first - rest), jnp.bfloat16)
        stack[first + rest : second, :] = jnp.zeros((second - first - rest, states), jnp.bfloat16)

    def put_rest():
        rounded = field[both:, :].astype(jnp.bfloat16)
        stack[first : first + rest, :] = rounded
        stack[second : second + rest, :] = rounded
        inner[...] = matmul(matrix[0:both, first:], stack[first:, :])

    def put_shared():
        rounded = field[0:both, :].astype(jnp.bfloat16)
        stack[0:both, :] = rounded
        stack[both:first, :] = rounded
        total = inner[...] + matmul(matrix[0:both, 0:first], stack[0:first, :])
        outgoing[...] = total
        rounded_out[...] = total.astype(jnp.bfloat16)

    def copies(slot):
        to_left = pltpu.make_async_remote_copy(
            src_ref=rounded_out.at[pl.ds(0, shared)],
            dst_ref=incoming.at[slot, pl.ds(shared, shared)],
            send_sem=sends.at[0],
            recv_sem=receives.at[slot, 0],
            device_id={"cell": left},
            device_id_type=MESH,
        )
        to_right = pltpu.make_async_remote_copy(
            src_ref=rounded_out.at[pl.ds(shared, shared)],
            dst_ref=incoming.at[slot, pl.ds(0, shared)],
            send_sem=sends.at[1],
            recv_sem=receives.at[slot, 1],
            device_id={"cell": right},
            device_id_type=MESH,
        )
        return to_left, to_right

    put_rest()
    ghost_copy.wait()
    field[shared:both, :] = ghost[...]
    put_shared()
    for copy in copies(0):
        copy.start()

    def vector(value):
        return jnp.full((1, states), value, jnp.float32)

    lowest, cut, upper = vector(bounds[0]), vector(bounds[1]), vector(bounds[2])
    half = (upper - cut) / 2.0
    centre = (upper + cut) / 2.0
    sigma_first = half / (lowest - centre)
    tau = 2.0 / sigma_first

    def step_rest(alpha, beta):
        new_rest = (
            matmul(matrix[both:, :], stack[...]) - centre * field[both:, :]
        ) * alpha - beta * before[both:, :]
        before[both:, :] = field[both:, :]
        field[both:, :] = new_rest

    def step_shared(step, alpha, beta):
        slot = lax.rem(step, 2)
        known = (
            outgoing[...] - centre * field[0:both, :]
        ) * alpha - beta * before[0:both, :]
        before[0:both, :] = field[0:both, :]
        for copy in copies(slot):
            copy.wait()
        field[0:both, :] = known + alpha * incoming[slot]
        put_shared()
        for copy in copies(lax.rem(step + 1, 2)):
            copy.start()

    def degree_step(step, carry):
        alpha, beta, sigma = carry
        step_rest(alpha, beta)
        put_rest()
        step_shared(step, alpha, beta)
        sigma_new = 1.0 / (tau - sigma)
        return 2.0 * sigma_new / half, sigma * sigma_new, sigma_new

    alpha, beta, _ = lax.fori_loop(
        0, DEGREE - 1, degree_step, (sigma_first / half, jnp.zeros_like(half), sigma_first)
    )

    def piece_copy(way, hop, piece, block, part):
        spot = (lows, low_ends)[part].at[block, pl.ds(piece * rows, rows)]
        return pltpu.make_async_remote_copy(
            src_ref=spot,
            dst_ref=spot,
            send_sem=along_send.at[way, hop, piece, part],
            recv_sem=along_recv.at[way, hop, piece, part],
            device_id={"state": lax.rem(place + 1 - 2 * way + groups, groups)},
            device_id_type=MESH,
        )

    def block_at(way, hop):
        return lax.rem(place - (1 - 2 * way) * hop + groups, groups)

    def hand_on(way, hop, piece, part):
        return piece_copy(way, hop, piece, block_at(way, hop), part)

    def arrival(way, hop, piece, part):
        return piece_copy(way, hop, piece, block_at(way, hop + 1), part)

    def sends_at(way, hop):
        if way == 0:
            return jnp.logical_and(place < groups - 1, place >= hop)
        return jnp.logical_and(place > 0, place + hop < groups)

    def receives_at(way, hop):
        if way == 0:
            return place >= hop + 1
        return place + hop + 1 < groups

    def send_own(part):
        for way in range(2):

            @pl.when(sends_at(way, 0))
            def _():
                for piece in range(owners):
                    hand_on(way, 0, piece, part).start()

    early = owned - 128
    step_rest(alpha, beta)
    lows[place] = field[both : both + early, :].T.astype(jnp.bfloat16)
    send_own(0)
    put_rest()
    step_shared(DEGREE - 1, alpha, beta)
    tail = jnp.concatenate([field[both + early :, :], field[0:shared, :]], axis=0)
    low_ends[place] = tail.T.astype(jnp.bfloat16)
    send_own(1)
    image[0:rest, :] = matmul(matrix[both:, :], stack[...]).astype(jnp.bfloat16)
    filtered[...] = jnp.concatenate([field[0:shared, :], field[both:, :]], axis=0).T
    last = DEGREE % 2
    for copy in copies(last):
        copy.wait()
    image[rest:, :] = (outgoing[0:shared, :] + incoming[last, 0:shared, :]).astype(jnp.bfloat16)

    def swap(block, piece):
        return pltpu.make_async_remote_copy(
            src_ref=parts.at[block, pl.ds(piece * rows, rows)],
            dst_ref=swapped.at[block, pl.ds(piece // 2 * rows, rows)],
            send_sem=swap_send.at[block, piece // 2],
            recv_sem=swap_recv.at[block, piece // 2],
            device_id={"cell": chip * 2 + 1 - core},
            device_id_type=MESH,
        )

    def owner_of(block, piece):
        return block * (owners // 2) + piece // 2

    def shipping(block, piece):
        return pltpu.make_async_remote_copy(
            src_ref=ship.at[block, pl.ds(piece // 2 * rows, rows)],
            dst_ref=gathered.at[chip],
            send_sem=ship_send.at[block, piece // 2],
            recv_sem=ship_recv.at[chip],
            device_id={"cell": 2 * owner_of(block, piece) + core},
            device_id_type=MESH,
        )

    def multiply(block, piece):
        here = slice(piece * rows, (piece + 1) * rows)
        parts[block, here, :] = matmul(lows[block, here, :], image[0:early, :]) + matmul(
            low_ends[block, here, :], image[early:, :]
        )

        @pl.when(core != piece % 2)
        def _():
            swap(block, piece).start()

    def pass_to_owner(block, piece):
        here = slice(piece * rows, (piece + 1) * rows)
        there = slice(piece // 2 * rows, (piece // 2 + 1) * rows)

        @pl.when(core == piece % 2)
        def _():
            swap(block, piece).wait_recv()
            total = parts[block, here, :] + swapped[block, there, :]

            @pl.when(owner_of(block, piece) == chip)
            def _():
                mine[...] = total

            @pl.when(owner_of(block, piece) != chip)
            def _():
                ship[block, there, :] = total
                shipping(block, piece).start()

    def pass_own():
        for piece in range(owners):
            pass_to_owner(place, piece)

    def pass_arrived(hop, piece):
        for way in range(2):

            @pl.when(receives_at(way, hop))
            def _():
                pass_to_owner(block_at(way, hop + 1), piece)

    for piece in range(owners):
        multiply(place, piece)
    waiting = [pass_own]
    for hop in range(groups - 1):
        for piece in range(owners):
            for way in range(2):

                @pl.when(receives_at(way, hop))
                def _():
                    for part in range(2):
                        arrival(way, hop, piece, part).wait_recv()
                        if hop + 1 < groups - 1:

                            @pl.when(sends_at(way, hop + 1))
                            def _():
                                hand_on(way, hop + 1, piece, part).start()

                    multiply(block_at(way, hop + 1), piece)

            for pending in waiting:
                pending()
            waiting = [functools.partial(pass_arrived, hop, piece)]
            if hop == groups - 2:
                waiting.pop()()
    for pending in waiting:
        pending()

    for way in range(2):
        for hop in range(groups - 1):

            @pl.when(sends_at(way, hop))
            def _():
                for piece in range(owners):
                    for part in range(2):
                        hand_on(way, hop, piece, part).wait_send()

    for block in range(groups):
        for piece in range(owners):

            @pl.when(core != piece % 2)
            def _():
                swap(block, piece).wait_send()

            @pl.when(jnp.logical_and(core == piece % 2, owner_of(block, piece) != chip))
            def _():
                shipping(block, piece).wait_send()

    for other in range(chips):

        @pl.when(other != chip)
        def _():
            pltpu.make_async_remote_copy(
                src_ref=gathered.at[other],
                dst_ref=gathered.at[other],
                send_sem=ship_send.at[0, 0],
                recv_sem=ship_recv.at[other],
                device_id={"cell": 2 * other + core},
                device_id_type=MESH,
            ).wait_recv()
            mine[...] += gathered[other]

    projected[...] = mine[...]


def filtered_block(start, links, cells, bounds, count, groups):
    states, owned = start.shape
    shared = owned // 8
    both = 2 * shared
    extent = owned + shared
    rest = extent - both
    depth = 2 * both + (rest + 127) // 128 * 128 + rest
    rows = states * groups // count
    pairs = states // rows // 2
    chips = count // 2
    vmem = pl.BlockSpec(memory_space=pltpu.VMEM)
    dma = pltpu.SemaphoreType.DMA
    return pl.pallas_call(
        functools.partial(filter_kernel, count, groups),
        out_shape=(
            jax.ShapeDtypeStruct((states, owned), jnp.float32),
            jax.ShapeDtypeStruct((rows, states), jnp.float32),
        ),
        in_specs=[vmem, vmem, vmem, pl.BlockSpec(memory_space=pltpu.SMEM)],
        out_specs=(vmem, vmem),
        scratch_shapes=[
            pltpu.VMEM((extent, depth), jnp.bfloat16),
            pltpu.VMEM((depth, states), jnp.bfloat16),
            pltpu.VMEM((extent, states), jnp.float32),
            pltpu.VMEM((extent, states), jnp.float32),
            pltpu.VMEM((both, states), jnp.float32),
            pltpu.VMEM((both, states), jnp.float32),
            pltpu.VMEM((both, states), jnp.bfloat16),
            pltpu.VMEM((2, both, states), jnp.bfloat16),
            pltpu.VMEM((shared, states), jnp.float32),
            pltpu.VMEM((owned, states), jnp.bfloat16),
            pltpu.VMEM((groups, states, owned - 128), jnp.bfloat16),
            pltpu.VMEM((groups, states, 128), jnp.bfloat16),
            pltpu.VMEM((groups, states, states), jnp.float32),
            pltpu.VMEM((groups, pairs * rows, states), jnp.float32),
            pltpu.VMEM((groups, pairs * rows, states), jnp.float32),
            pltpu.VMEM((chips, rows, states), jnp.float32),
            pltpu.VMEM((rows, states), jnp.float32),
            dma((2,)),
            dma((2, 2)),
            dma((2,)),
            dma((2, groups, 2 * pairs, 2)),
            dma((2, groups, 2 * pairs, 2)),
            dma((groups, pairs)),
            dma((groups, pairs)),
            dma((groups, pairs)),
            dma((chips,)),
        ],
        compiler_params=pltpu.CompilerParams(
            collective_id=0, has_side_effects=True, vmem_limit_bytes=40 * 1024 * 1024
        ),
    )(start, links, cells, bounds)


def solution(mesh):
    in_specs = (P("state", "cell"), P("cell", None), P("cell", None, None), P())
    out_specs = (P("state", "cell"), P("cell", "state"))
    return jax.shard_map(
        functools.partial(
            filtered_block, count=mesh.shape["cell"], groups=mesh.shape["state"]
        ),
        mesh=mesh, in_specs=in_specs, out_specs=out_specs, check_vma=False,
    )
```
